128 devices in a mesh: seq: 4 (over z_hi, core), shard: 32 (over y, x, z_lo).
Axes of the slice: x: 4, y: 4, z: 4 (z_hi: 2, z_lo: 2; z = z_hi * 2 + z_lo), core: 2. Of those that a mesh axis runs over, the one named last changes fastest.
Arguments:
- hidden_in: bfloat16 [16384, 1024], P(('seq', 'shard')), may hold values from -6 to 6
- positions: int32 [16384], P(('seq', 'shard')), may hold values from 1 to 16383, as said below
- first_gain: bfloat16 [1024], P('shard'), may hold values from 0.5 to 1.5
- first_shift: bfloat16 [1024], P('shard'), may hold values from -0.5 to 0.5
- second_gain: bfloat16 [1024], P('shard'), may hold values from 0.5 to 1.5
- second_shift: bfloat16 [1024], P('shard'), may hold values from -0.5 to 0.5
- joined_weight: bfloat16 [1024, 3072], P('shard'), may hold values from -0.1875 to 0.1875
- joined_bias: bfloat16 [1024, 3], P('shard'), may hold values from -0.049804688 to 0.049804688
- output_weight: bfloat16 [1024, 1024], P('shard'), may hold values from -0.75 to 0.75
- output_bias: bfloat16 [1024], P('shard'), may hold values from -0.5 to 0.5
- up_weight: bfloat16 [1024, 4096], P('shard'), may hold values from -0.1875 to 0.1875
- up_bias: bfloat16 [4096], P('shard'), may hold values from -0.5 to 0.5
- down_weight: bfloat16 [4096, 1024], P('shard'), may hold values from -0.09375 to 0.09375
- down_bias: bfloat16 [1024], P('shard'), may hold values from -0.5 to 0.5
- cotangent: bfloat16 [16384, 1024], P(('seq', 'shard')), may hold values from -6 to 6
Outputs:
- block_out: bfloat16 [16384, 1024], P(('seq', 'shard'))
- input_grad: bfloat16 [16384, 1024], P(('seq', 'shard'))
- first_gain_grad: float32 [1024], P('shard')
- first_shift_grad: float32 [1024], P('shard')
- second_gain_grad: float32 [1024], P('shard')
- second_shift_grad: float32 [1024], P('shard')
- joined_weight_grad: float32 [1024, 3072], P('shard')
- joined_bias_grad: float32 [1024, 3], P('shard')
- output_weight_grad: float32 [1024, 1024], P('shard')
- output_bias_grad: float32 [1024], P('shard')
- up_weight_grad: float32 [1024, 4096], P('shard')
- up_bias_grad: float32 [4096], P('shard')
- down_weight_grad: float32 [4096, 1024], P('shard')
- down_bias_grad: float32 [1024], P('shard')
The draws below stay inside these ranges and needn't reach their ends.
Inputs may be any that keep to these rules, and one draw needn't show every extreme that they name: Within each of the 2 sequences of 8192 consecutive tokens the positions rise by 1 or 2 from one token to the next, and the last token of every sequence has position 16383.
All inputs are finite; a program needn't handle non-finite values.
Results may differ from the reference program's by a relative error of at most 0.025.
Values may be sent and summed in bfloat16 or wider, within the bound.
No kernel may reach another device: no remote copies, remote signals or barrier semaphores. Data moves between devices by JAX's collectives and lax.ppermute only.
A program may use at most 256 MiB of HBM per device.

```python
import math
import jax
import jax.numpy as jnp
from jax import lax

D = 1024
FF = 4096
HEAD_DIM = 64
ROTARY = 16
SEQS = 2
TOKENS = 16384
LENGTH = 8192


def draw_positions(key, part):
    key = jax.random.fold_in(key, 11)
    steps = jax.random.randint(key, (SEQS, LENGTH), 1, 3, dtype=jnp.int32)
    after = jnp.flip(jnp.cumsum(jnp.flip(steps, 1), axis=1), 1) - steps
    return (2 * LENGTH - 1 - after).reshape(-1).astype(jnp.int32)


def steps_of(own_key, shape, cuts, low, high):
    loudness = 1.0
    for position, blocks in cuts:
        draws = jax.random.uniform(jax.random.fold_in(jax.random.fold_in(own_key, 6), position), (blocks,), jnp.float32, low / len(cuts), high / len(cuts))
        loudness = loudness * jnp.repeat(jnp.exp(draws), shape[position] // blocks).reshape((-1,) + (1,) * (len(shape) - 1 - position))
    return loudness


def scatter_about(rng, extent, scale, limit, cuts=(), kind=jnp.bfloat16):
    values = scale * jax.random.normal(rng, extent, jnp.float32)
    if cuts:
        values = values * steps_of(rng, extent, cuts, -0.22, 0.18)
    return jnp.clip(values, -limit, limit).astype(kind)


def setup_inputs(seed: int = 0) -> dict:
    arg_keys = jax.random.split(jax.random.key(seed), 16)
    return {
        "hidden_in": scatter_about(arg_keys[0], (TOKENS, D), 1.0, 6.0, ((0, 128),)),
        "positions": draw_positions(jax.random.fold_in(arg_keys[15], 71), 0),
        "first_gain": jnp.clip(1.0 + 0.1 * jax.random.normal(arg_keys[2], (D,), jnp.float32), 0.5, 1.5).astype(jnp.bfloat16),
        "first_shift": jnp.clip(jax.random.uniform(arg_keys[3], (D,), jnp.float32, -0.5, 0.5) * steps_of(arg_keys[3], (D,), ((0, 32),), -0.4, 0.0), -0.5, 0.5).astype(jnp.bfloat16),
        "second_gain": jnp.clip(1.0 + 0.1 * jax.random.normal(arg_keys[4], (D,), jnp.float32), 0.5, 1.5).astype(jnp.bfloat16),
        "second_shift": jnp.clip(jax.random.uniform(arg_keys[5], (D,), jnp.float32, -0.5, 0.5) * steps_of(arg_keys[5], (D,), ((0, 32),), -0.4, 0.0), -0.5, 0.5).astype(jnp.bfloat16),
        "joined_weight": scatter_about(arg_keys[6], (D, 3 * D), D ** -0.5, 0.1875, ((0, 32),)),
        "joined_bias": jnp.clip(jax.random.uniform(arg_keys[7], (D, 3), jnp.float32, -0.049804688, 0.049804688) * steps_of(arg_keys[7], (D, 3), ((0, 32),), -0.4, 0.0), -0.049804688, 0.049804688).astype(jnp.bfloat16),
        "output_weight": scatter_about(arg_keys[8], (D, D), (D // 16) ** -0.5, 0.75, ((0, 32),)),
        "output_bias": jnp.clip(jax.random.uniform(arg_keys[9], (D,), jnp.float32, -0.5, 0.5) * steps_of(arg_keys[9], (D,), ((0, 32),), -0.4, 0.0), -0.5, 0.5).astype(jnp.bfloat16),
        "up_weight": scatter_about(arg_keys[10], (D, FF), D ** -0.5, 0.1875, ((0, 32),)),
        "up_bias": jnp.clip(jax.random.uniform(arg_keys[11], (FF,), jnp.float32, -0.5, 0.5) * steps_of(arg_keys[11], (FF,), ((0, 32),), -0.4, 0.0), -0.5, 0.5).astype(jnp.bfloat16),
        "down_weight": scatter_about(arg_keys[12], (FF, D), FF ** -0.5, 0.09375, ((0, 32),)),
        "down_bias": jnp.clip(jax.random.uniform(arg_keys[13], (D,), jnp.float32, -0.5, 0.5) * steps_of(arg_keys[13], (D,), ((0, 32),), -0.4, 0.0), -0.5, 0.5).astype(jnp.bfloat16),
        "cotangent": scatter_about(arg_keys[14], (TOKENS, D), 1.0, 6.0, ((0, 128),)),
    }


@jax.custom_vjp
def low(v):
    return lax.optimization_barrier(v.astype(jnp.bfloat16)).astype(jnp.float32)

@jax.custom_vjp
def low_back(v):
    return v

def low_keep(v):
    return (low(v), None)

def low_pass(kept, grad):
    return (grad,)

def back_keep(v):
    return (v, None)

def back_low(kept, grad):
    return (low(grad),)
low.defvjp(low_keep, low_pass)
low_back.defvjp(back_keep, back_low)
EPS = 1e-05
NEG = -1e+30
HIGH = lax.Precision.HIGHEST

def product(left, right):
    return jnp.dot(left, right, precision=HIGH)

def layer_norm(values, gain, shift):
    mean = lax.optimization_barrier(jnp.mean(values, axis=-1, keepdims=True))
    centered = values - mean
    scaled = centered * lax.rsqrt(lax.optimization_barrier(jnp.mean(centered * centered, axis=-1, keepdims=True)) + EPS)
    return scaled * gain + shift

def rotary_tables(positions):
    inv_freq = 1.0 / 10000.0 ** (jnp.arange(0, ROTARY, 2, dtype=jnp.float32) / ROTARY)
    angles = positions.astype(jnp.float32)[:, None] * inv_freq[None, :]
    angles = jnp.concatenate([angles, angles], axis=1)
    return (jnp.cos(angles), jnp.sin(angles))

def rotate(values, cosine, sine):
    turned = values[..., :ROTARY]
    half = ROTARY // 2
    swapped = jnp.concatenate([-turned[..., half:], turned[..., :half]], axis=-1)
    turned = turned * cosine[:, None, :] + swapped * sine[:, None, :]
    return jnp.concatenate([turned, values[..., ROTARY:]], axis=-1)

def attend_sequence(query, keys, values):
    block = math.gcd(512, LENGTH)
    count = LENGTH // block
    heads = query.shape[1]
    scale = HEAD_DIM ** (-0.5)
    key_index = jnp.arange(LENGTH, dtype=jnp.int32)

    def one_block(operands):
        rows_here, first = operands
        scores = jnp.einsum('qhd,khd->hqk', rows_here, keys, precision=HIGH) * scale
        scores = low_back(scores)
        allowed = key_index[None, :] <= (first + jnp.arange(block, dtype=jnp.int32))[:, None]
        scores = jnp.where(allowed[None], scores, NEG)
        weights = low(jax.nn.softmax(scores, axis=-1))
        return jnp.einsum('hqk,khd->qhd', weights, values, precision=HIGH)
    grouped = query.reshape(count, block, heads, HEAD_DIM)
    firsts = (jnp.arange(count, dtype=jnp.int32) * block).astype(jnp.int32)
    outputs = lax.map(jax.checkpoint(one_block), (grouped, firsts))
    return outputs.reshape(LENGTH, heads, HEAD_DIM)

def forward(hidden, gain_one, shift_one, gain_two, shift_two, joined_w, joined_b, out_w, out_b, up_w, up_b, down_w, down_b, cosine, sine):
    width = hidden.shape[1]
    heads = width // HEAD_DIM
    first_in = low(layer_norm(hidden, gain_one, shift_one))
    second_in = low(layer_norm(hidden, gain_two, shift_two))
    joined = low_back(product(first_in, joined_w) + jnp.transpose(joined_b).reshape(-1))
    joined = joined.reshape(-1, 3, heads, HEAD_DIM)
    query = low(low_back(rotate(joined[:, 0], cosine, sine)))
    keys = low(low_back(rotate(joined[:, 1], cosine, sine)))
    values = low(low_back(joined[:, 2]))
    pieces = []
    for index in range(SEQS):
        lower = index * LENGTH
        upper = lower + LENGTH
        pieces.append(attend_sequence(query[lower:upper], keys[lower:upper], values[lower:upper]))
    mixed = jnp.concatenate(pieces, axis=0).reshape(-1, width)
    mixed = low(low_back(mixed))
    attention = product(mixed, out_w) + out_b
    up_pre = low_back(product(second_in, up_w) + up_b)
    activated = low(jax.nn.gelu(up_pre, approximate=False))
    feed = product(activated, down_w) + down_b
    return hidden + attention + feed

def reference(hidden_in, positions, first_gain, first_shift, second_gain, second_shift, joined_weight, joined_bias, output_weight, output_bias, up_weight, up_bias, down_weight, down_bias, cotangent):
    cosine, sine = rotary_tables(positions)
    params = tuple((item.astype(jnp.float32) for item in (hidden_in, first_gain, first_shift, second_gain, second_shift, joined_weight, joined_bias, output_weight, output_bias, up_weight, up_bias, down_weight, down_bias)))

    def wrapped(*operands):
        return forward(*operands, cosine, sine)
    block_out, pullback = jax.vjp(wrapped, *params)
    grads = pullback(cotangent.astype(jnp.float32))
    return (block_out.astype(jnp.bfloat16), grads[0].astype(jnp.bfloat16), grads[1], grads[2], grads[3], grads[4], grads[5], grads[6], grads[7], grads[8], grads[9], grads[10], grads[11], grads[12])
```

```python
import jax
import jax.numpy as jnp
import numpy as np
from jax import lax
from jax.experimental import pallas as pl
from jax.experimental.pallas import tpu as pltpu
from jax.sharding import Mesh
from jax.sharding import PartitionSpec as P

HEAD_DIM = 64
ROTARY = 16
EPS = 1e-05
NEG = -1e30
HIGH = lax.Precision.HIGHEST
MIDDLE = lax.Precision.HIGH
BF = jnp.bfloat16
F32 = jnp.float32
ROW = 128
QT = 512
KT = 512
AXES = ("zh", "c", "y", "x", "zl")
PLANE = ("x", "zl")
SHARD = ("y", "x", "zl")


def attention_kernel(which, msg, out, kv, kvt, qg, qz, gz, dkv):
    sources, blocks = msg.shape[0], msg.shape[1]
    chunks = blocks - 2
    span = sources * ROW
    low_rows = lax.broadcasted_iota(jnp.int32, (2 * HEAD_DIM, ROW), 0) < HEAD_DIM
    low_lanes = lax.broadcasted_iota(jnp.int32, (ROW, 2 * HEAD_DIM), 1) < HEAD_DIM

    def key_place(source, place):
        chunk = lax.rem(place + which[1] * (chunks // 2), chunks)
        return pl.multiple_of(chunk * span + source * ROW, ROW)

    def load_keys(index, carry):
        source, place = index // chunks, index % chunks
        at = key_place(source, place)
        block = msg[source, place]
        kv[pl.ds(at, ROW), :] = block
        kvt[:, pl.ds(at, ROW)] = block.astype(F32).T.astype(BF)
        dkv[pl.ds(at, ROW), :] = jnp.zeros((ROW, 2 * HEAD_DIM), F32)
        return carry

    lax.fori_loop(0, sources * chunks, load_keys, 0)

    def load_queries(index, carry):
        source, part = index // 2, index % 2
        at = pl.multiple_of(part * span + source * ROW, ROW)
        block = msg[source, chunks + part].astype(F32)
        block = jnp.where(low_lanes, block * (HEAD_DIM**-0.5), block)
        qg[pl.ds(at, ROW), :] = block.astype(BF)
        turned = block.T
        qz[:, pl.ds(at, ROW)] = jnp.where(low_rows, turned, 0.0).astype(BF)
        gz[:, pl.ds(at, ROW)] = jnp.where(low_rows, 0.0, turned).astype(BF)
        return carry

    lax.fori_loop(0, sources * 2, load_queries, 0)
    tiles = span // QT
    lanes_tile = lax.broadcasted_iota(jnp.int32, (QT, 2 * HEAD_DIM), 1) < HEAD_DIM
    causal = lax.broadcasted_iota(jnp.int32, (KT, QT), 0) <= lax.broadcasted_iota(
        jnp.int32, (KT, QT), 1
    )

    def one_tile(index, carry):
        part, tile = index // tiles, index % tiles
        chunk = jnp.where(part == which[1], which[0], chunks - 1 - which[0])
        at = pl.multiple_of(index * QT, QT)
        full = chunk * (span // KT) + tile
        query_t = qz[:, pl.ds(at, QT)]
        grad_t = gz[:, pl.ds(at, QT)]

        def forward(step, state, masked):
            best, total, summed = state
            k_at = pl.multiple_of(step * KT, KT)
            scores = jnp.dot(kv[pl.ds(k_at, KT), :], query_t, preferred_element_type=F32)
            if masked:
                scores = jnp.where(causal, scores, NEG)
            new_best = jnp.maximum(best, jnp.max(scores, axis=0, keepdims=True))
            probs = jnp.exp(scores - new_best)
            factor = jnp.exp(best - new_best)
            total = total * factor + jnp.sum(probs, axis=0, keepdims=True)
            summed = summed * factor + jnp.dot(
                kvt[HEAD_DIM:, pl.ds(k_at, KT)], probs.astype(BF), preferred_element_type=F32
            )
            return new_best, total, summed

        state = (
            jnp.full((1, QT), NEG, F32),
            jnp.zeros((1, QT), F32),
            jnp.zeros((HEAD_DIM, QT), F32),
        )
        state = lax.fori_loop(0, full, lambda s, v: forward(s, v, False), state)
        best, total, summed = forward(full, state, True)
        mixed = (summed / total).astype(BF).astype(F32)
        log_rows = best + jnp.log(total)
        delta = jnp.sum(mixed * grad_t[HEAD_DIM:, :].astype(F32), axis=0, keepdims=True)
        both = qg[pl.ds(at, QT), :]
        zero = jnp.zeros_like(both)
        only_query = jnp.where(lanes_tile, both, zero)
        only_grad = jnp.where(lanes_tile, zero, both)

        def backward(step, grad_query, masked):
            k_at = pl.multiple_of(step * KT, KT)
            block = kv[pl.ds(k_at, KT), :]
            scores = jnp.dot(block, query_t, preferred_element_type=F32)
            probs = jnp.exp(scores - log_rows)
            if masked:
                probs = jnp.where(causal, probs, 0.0)
            grad_probs = jnp.dot(block, grad_t, preferred_element_type=F32)
            grad_scores = (probs * (grad_probs - delta)).astype(BF)
            dkv[pl.ds(k_at, KT), :] += jnp.dot(
                grad_scores, only_query, preferred_element_type=F32
            ) + jnp.dot(probs.astype(BF), only_grad, preferred_element_type=F32)
            return grad_query + jnp.dot(
                kvt[:HEAD_DIM, pl.ds(k_at, KT)], grad_scores, preferred_element_type=F32
            )

        grad_query = jnp.zeros((HEAD_DIM, QT), F32)
        grad_query = lax.fori_loop(0, full, lambda s, v: backward(s, v, False), grad_query)
        grad_query = backward(full, grad_query, True) * (HEAD_DIM**-0.5)
        result = jnp.concatenate([grad_query, mixed], axis=0).T.astype(BF)
        for piece in range(QT // ROW):
            out[tile * (QT // ROW) + piece, chunks + part] = result[
                piece * ROW : (piece + 1) * ROW
            ]
        return carry

    lax.fori_loop(0, 2 * tiles, one_tile, 0)

    def store_keys(index, carry):
        source, place = index // chunks, index % chunks
        out[source, place] = dkv[pl.ds(key_place(source, place), ROW), :].astype(BF)
        return carry

    lax.fori_loop(0, sources * chunks, store_keys, 0)


def attend(message, which):
    sources, blocks = message.shape[0], message.shape[1]
    keys = sources * (blocks - 2) * ROW
    queries = sources * 2 * ROW
    wide = 2 * HEAD_DIM
    pairs = keys * queries * 9 // 16
    return pl.pallas_call(
        attention_kernel,
        out_shape=jax.ShapeDtypeStruct(message.shape, BF),
        in_specs=[
            pl.BlockSpec(memory_space=pltpu.SMEM),
            pl.BlockSpec(memory_space=pltpu.VMEM),
        ],
        out_specs=pl.BlockSpec(memory_space=pltpu.VMEM),
        scratch_shapes=[
            pltpu.VMEM((keys, wide), BF),
            pltpu.VMEM((wide, keys), BF),
            pltpu.VMEM((queries, wide), BF),
            pltpu.VMEM((wide, queries), BF),
            pltpu.VMEM((wide, queries), BF),
            pltpu.VMEM((keys, wide), F32),
        ],
        compiler_params=pltpu.CompilerParams(vmem_limit_bytes=48 * 1024 * 1024),
        cost_estimate=pl.CostEstimate(
            flops=pairs * 14 * HEAD_DIM,
            bytes_accessed=4 * sources * blocks * ROW * wide,
            transcendentals=2 * pairs,
        ),
        name="attention",
    )(which, message)


def front_kernel(
    which, own, far, table, bias, cosine, sine, w_joined, w_out, msg, first, second, scaled, grads
):
    step = pl.program_id(0)
    steps = pl.num_programs(0)
    rows = 2 * ROW
    width = own.shape[2]
    wide = 2 * HEAD_DIM
    quarters = own.shape[0] * steps // 2
    here = step < steps // 2
    values = jnp.where(here, own[:, :ROW], far[:, :ROW]).reshape(rows, width).astype(F32)
    cots = jnp.where(here, own[:, ROW : 2 * ROW], far[:, ROW : 2 * ROW]).reshape(rows, width)
    grads[...] = cots
    centered = values - jnp.mean(values, axis=-1, keepdims=True)
    variance = jnp.mean(centered * centered, axis=-1, keepdims=True)
    normal = centered * lax.rsqrt(variance + EPS)
    scaled[...] = normal
    first_in = (normal * table[0:1, :] + table[1:2, :]).astype(BF)
    first[...] = first_in
    second[...] = (normal * table[2:3, :] + table[3:4, :]).astype(BF)
    joined = jnp.dot(first_in, w_joined[...], preferred_element_type=F32) + bias[...]
    grad_mixed = lax.dot_general(
        cots, w_out[...], (((1,), (1,)), ((), ())), preferred_element_type=F32
    )
    lane = lax.broadcasted_iota(jnp.int32, (rows, wide), 1)
    half = ROTARY // 2
    for block in range(4):
        piece = joined[:, block * wide : (block + 1) * wide]
        turned = jnp.where(
            lane < half, -pltpu.roll(piece, wide - half, 1), pltpu.roll(piece, half, 1)
        )
        piece = piece * cosine[...] + turned * sine[...]
        head = block % 2
        if block >= 2:
            piece = jnp.where(lane < HEAD_DIM, piece, grad_mixed[:, head * wide : (head + 1) * wide])
        piece = piece.astype(BF)
        for i in range(2):
            place = step * 2 + i
            part = piece[i * ROW : (i + 1) * ROW]
            if block < 2:
                for quarter in range(quarters):
                    msg[quarter * 2 + head, place] = part
            else:
                later = jnp.where(here, 0, 1)
                plane = place - later * quarters
                chunk = jnp.where(later == which[1], plane, quarters - 1 - plane)
                msg[chunk * 2 + head, 2 * quarters + later] = part


def front(which, own, far, table, bias, cosine, sine, w_joined, w_out):
    planes, payload_rows, width = own.shape
    steps = planes
    rows = 2 * ROW
    tokens = 2 * planes * ROW
    wide = 2 * HEAD_DIM

    def whole(array):
        return pl.BlockSpec(array.shape, lambda s: (0,) * array.ndim)

    def rowed(columns):
        return pl.BlockSpec((rows, columns), lambda s: (s, 0))

    msg_shape = (2 * planes, 2 * planes + 2, ROW, wide)
    return pl.pallas_call(
        front_kernel,
        grid=(steps,),
        out_shape=(
            jax.ShapeDtypeStruct(msg_shape, BF),
            jax.ShapeDtypeStruct((tokens, width), BF),
            jax.ShapeDtypeStruct((tokens, width), BF),
            jax.ShapeDtypeStruct((tokens, width), F32),
            jax.ShapeDtypeStruct((tokens, width), BF),
        ),
        in_specs=[
            pl.BlockSpec(memory_space=pltpu.SMEM),
            pl.BlockSpec((2, payload_rows, width), lambda s: (jnp.minimum(s, steps // 2 - 1), 0, 0)),
            pl.BlockSpec((2, payload_rows, width), lambda s: (jnp.maximum(s - steps // 2, 0), 0, 0)),
            whole(table),
            whole(bias),
            rowed(wide),
            rowed(wide),
            whole(w_joined),
            whole(w_out),
        ],
        out_specs=(
            pl.BlockSpec(msg_shape, lambda s: (0, 0, 0, 0)),
            rowed(width),
            rowed(width),
            rowed(width),
            rowed(width),
        ),
        compiler_params=pltpu.CompilerParams(vmem_limit_bytes=48 * 1024 * 1024),
        cost_estimate=pl.CostEstimate(
            flops=2 * tokens * width * 6 * wide, bytes_accessed=24 * tokens * width, transcendentals=0
        ),
        name="front",
    )(which, own, far, table, bias, cosine, sine, w_joined, w_out)


def back_kernel(
    which,
    ans,
    table,
    cosine,
    sine,
    w_joined,
    w_out,
    first,
    scaled,
    grads,
    feed,
    second,
    block_out,
    scaled_out,
    joined_grad,
    out_grad,
    sums,
):
    step = pl.program_id(0)
    wide = 2 * HEAD_DIM
    quarters = ans.shape[0] // 2
    rows = 2 * ROW
    lane = lax.broadcasted_iota(jnp.int32, (rows, wide), 1)
    half = ROTARY // 2

    @pl.when(step == 0)
    def _():
        joined_grad[...] = jnp.zeros_like(joined_grad)
        out_grad[...] = jnp.zeros_like(out_grad)
        sums[...] = jnp.zeros_like(sums)

    def turned_back(piece):
        shifted = piece * sine[...]
        shifted = jnp.where(
            lane < half,
            pltpu.roll(shifted, wide - half, 1),
            jnp.where(lane < ROTARY, -pltpu.roll(shifted, half, 1), 0.0),
        )
        return piece * cosine[...] + shifted

    key_value, mixed, query = [], [], []
    for head in range(2):
        pair, other = [], []
        for i in range(2):
            place = step * 2 + i
            total = ans[head, place].astype(F32)
            for quarter in range(1, quarters):
                total = total + ans[quarter * 2 + head, place].astype(F32)
            pair.append(total)
            later = place // quarters
            plane = place - later * quarters
            chunk = jnp.where(later == which[1], plane, quarters - 1 - plane)
            other.append(ans[chunk * 2 + head, 2 * quarters + later])
        total = jnp.concatenate(pair, axis=0).astype(BF).astype(F32)
        key_value.append(turned_back(total).astype(BF))
        other = jnp.concatenate(other, axis=0)
        mixed.append(other)
        turned = turned_back(other.astype(F32))
        query.append(jnp.where(lane < HEAD_DIM, turned, 0.0).astype(BF))
    joined = jnp.concatenate(key_value + query, axis=1)
    mixed = jnp.concatenate(mixed, axis=1)
    cots = grads[...]
    attention = jnp.dot(mixed, w_out[...], preferred_element_type=F32)
    block_out[...] = (feed[...] + attention).astype(BF)
    grad_first = lax.dot_general(
        joined, w_joined[...], (((1,), (1,)), ((), ())), preferred_element_type=F32
    )
    grad_second = second[...]
    normal = scaled[...]
    scaled_out[...] = (grad_first * table[0:1, :] + grad_second * table[2:3, :]).astype(BF)
    over_tokens = (((0,), (0,)), ((), ()))
    joined_grad[...] += lax.dot_general(
        first[...], joined, over_tokens, preferred_element_type=F32
    )
    out_grad[...] += lax.dot_general(mixed, cots, over_tokens, preferred_element_type=F32)
    sums[0:1, :] += jnp.sum(grad_first * normal, axis=0, keepdims=True)
    sums[1:2, :] += jnp.sum(grad_first, axis=0, keepdims=True)
    sums[2:3, :] += jnp.sum(grad_second * normal, axis=0, keepdims=True)
    sums[3:4, :] += jnp.sum(grad_second, axis=0, keepdims=True)
    sums[4:5, : 4 * wide] += jnp.sum(joined.astype(F32), axis=0, keepdims=True)


def back(which, ans, table, cosine, sine, w_joined, w_out, first, scaled, grads, feed, second):
    tokens, width = scaled.shape
    rows = 2 * ROW
    wide = 2 * HEAD_DIM

    def whole(shape):
        return pl.BlockSpec(shape, lambda s: (0,) * len(shape))

    def rowed(columns):
        return pl.BlockSpec((rows, columns), lambda s: (s, 0))

    return pl.pallas_call(
        back_kernel,
        grid=(tokens // rows,),
        out_shape=(
            jax.ShapeDtypeStruct((tokens, width), BF),
            jax.ShapeDtypeStruct((tokens, width), BF),
            jax.ShapeDtypeStruct(w_joined.shape, F32),
            jax.ShapeDtypeStruct(w_out.shape, F32),
            jax.ShapeDtypeStruct((8, width), F32),
        ),
        in_specs=[pl.BlockSpec(memory_space=pltpu.SMEM), whole(ans.shape), whole(table.shape)]
        + [rowed(wide)] * 2
        + [whole(w_joined.shape), whole(w_out.shape)]
        + [rowed(width)] * 5,
        out_specs=(
            rowed(width),
            rowed(width),
            whole(w_joined.shape),
            whole(w_out.shape),
            whole((8, width)),
        ),
        compiler_params=pltpu.CompilerParams(vmem_limit_bytes=48 * 1024 * 1024),
        cost_estimate=pl.CostEstimate(
            flops=2 * tokens * width * 12 * wide, bytes_accessed=24 * tokens * width, transcendentals=0
        ),
        name="back",
    )(which, ans, table, cosine, sine, w_joined, w_out, first, scaled, grads, feed, second)


def settle_kernel(which, mine, other, joined, up, down, out, vectors):
    shard_rows, wide = joined.shape[0], 2 * HEAD_DIM
    planes = up.shape[1] // 1024
    up_cols = up.shape[1] // (2 * planes)
    width = joined.shape[1] // 3
    lane = lax.broadcasted_iota(jnp.int32, (shard_rows, wide), 1) < HEAD_DIM
    total = jnp.zeros((shard_rows, wide), F32)
    first = which[1] == 0
    pair = (
        jnp.where(first, mine[...], other[...]),
        jnp.where(first, other[...], mine[...]),
    )
    side = planes // 2 * shard_rows
    for core in range(2):
        source = pair[core]
        for plane in range(planes):
            top = plane % 2 * shard_rows
            left = plane // 2 * up_cols
            blocks = [
                source[top : top + shard_rows, left + i * wide : left + (i + 1) * wide]
                for i in range(4)
            ]
            at = (2 * plane + core) * wide
            swapped = [pltpu.roll(block, HEAD_DIM, 1) for block in blocks]
            joined[:, at : at + wide] = jnp.where(lane, blocks[2], swapped[3])
            joined[:, width + at : width + at + wide] = jnp.where(lane, blocks[0], swapped[1])
            joined[:, 2 * width + at : 2 * width + at + wide] = jnp.where(
                lane, swapped[0], blocks[1]
            )
            total = total + blocks[2]
            at = (2 * plane + core) * up_cols
            up[:, at : at + up_cols] = source[
                side + top : side + top + shard_rows, left : left + up_cols
            ]
        half = down.shape[0] // 2
        down[core * half : (core + 1) * half, :] = source[2 * side : 2 * side + half]
        start = 2 * side + half
        half = out.shape[0] // 2
        out[core * half : (core + 1) * half, :] = source[start : start + half]
    vectors[...] = pltpu.roll(total, HEAD_DIM, 1)


def settle(which, mine, other, shapes):
    vmem = pl.BlockSpec(memory_space=pltpu.VMEM)
    return pl.pallas_call(
        settle_kernel,
        out_shape=tuple(jax.ShapeDtypeStruct(shape, F32) for shape in shapes),
        in_specs=[pl.BlockSpec(memory_space=pltpu.SMEM), vmem, vmem],
        out_specs=(vmem,) * len(shapes),
        compiler_params=pltpu.CompilerParams(vmem_limit_bytes=24 * 1024 * 1024),
        name="settle",
    )(which, mine, other)


def exchange(values, names):
    return lax.all_to_all(values, names, split_axis=0, concat_axis=0, tiled=True)


def core_swap(values):
    return lax.ppermute(values, "c", [(0, 1), (1, 0)])


def ring_shifts(size):
    return (1, size - 1, *range(2, size - 1))


def ring_move(values, names, size, shift):
    return lax.ppermute(values, names, [(i, (i + shift) % size) for i in range(size)])


def pin(*values):
    return lax.optimization_barrier(values)


def in_order(core, own, other):
    return jnp.where(core == 0, own, other), jnp.where(core == 0, other, own)


def normalize(values):
    mean = jnp.mean(values, axis=-1, keepdims=True)
    centered = values - mean
    inverse = lax.rsqrt(jnp.mean(centered * centered, axis=-1, keepdims=True) + EPS)
    return centered * inverse, inverse


def rotary_constants():
    half = ROTARY // 2
    wide = 2 * HEAD_DIM
    turn = np.zeros((wide, wide), np.float32)
    spread = np.zeros((half, wide), np.float32)
    keep = np.ones((wide,), np.float32)
    for i in range(half):
        turn[half + i, i] = -1.0
        turn[i, half + i] = 1.0
        spread[i, i] = 1.0
        spread[i, half + i] = 1.0
    keep[:ROTARY] = 0.0
    return turn, spread, keep


def per_device(
    hidden_in,
    positions,
    first_gain,
    first_shift,
    second_gain,
    second_shift,
    joined_weight,
    joined_bias,
    output_weight,
    output_bias,
    up_weight,
    up_bias,
    down_weight,
    down_bias,
    cotangent,
):
    rows, width = hidden_in.shape
    shard_rows = joined_weight.shape[0]
    hidden_width = up_weight.shape[1]
    wide_rows = down_weight.shape[0]
    planes = lax.axis_size("y")
    quarters = lax.axis_size("x")
    peers = quarters * lax.axis_size("zl")
    core = lax.axis_index("c")
    plane = lax.axis_index("y")
    tokens = 2 * planes * rows
    up_cols = hidden_width // (2 * planes)
    head_cols = width // (2 * planes)
    slice_index = 2 * plane + core

    whole = positions // 128
    pos_rows = jnp.stack([whole, positions - whole * 128]).astype(BF)
    pos_rows = jnp.pad(pos_rows, ((0, 14), (0, width - rows)))
    payload = jnp.concatenate([hidden_in, cotangent, pos_rows], axis=0)
    payload = exchange(jnp.broadcast_to(payload[None], (planes,) + payload.shape), "y")

    def pair_up(left, right):
        return jnp.concatenate([left, right], axis=-1)

    wj = lax.dynamic_index_in_dim(
        joined_weight.reshape(shard_rows, 3, planes, 2, 2, HEAD_DIM), core, 3, keepdims=False
    )
    vectors = jnp.concatenate(
        [
            jnp.stack(
                [first_gain, first_shift, second_gain, second_shift, output_bias, down_bias], axis=1
            ),
            joined_bias,
            up_bias.reshape(shard_rows, -1),
        ],
        axis=1,
    )
    vectors = jnp.pad(vectors, ((0, 0), (0, HEAD_DIM - vectors.shape[1])))
    vectors = jnp.broadcast_to(vectors[:, None, None], (shard_rows, planes, 2, HEAD_DIM))
    columns = jnp.concatenate([pair_up(wj[:, 1], wj[:, 2]), pair_up(wj[:, 0], vectors)], axis=2)
    columns = jnp.transpose(columns, (1, 0, 2, 3)).reshape(planes, shard_rows, -1)
    wu = lax.dynamic_index_in_dim(
        up_weight.reshape(shard_rows, planes, 2, up_cols), core, 2, keepdims=False
    )
    columns = jnp.concatenate([columns, jnp.transpose(wu, (1, 0, 2))], axis=2)
    half_out, half_down = shard_rows // 2, wide_rows // 2

    def spread_columns(columns):
        message = jnp.broadcast_to(columns[:, None], (planes, peers) + columns.shape[1:])
        message = exchange(message.reshape((planes * peers,) + columns.shape[1:]), SHARD)
        return message.reshape(width, -1)

    rows_half = jnp.concatenate(
        [
            lax.dynamic_slice_in_dim(output_weight, core * half_out, half_out, 0),
            lax.dynamic_slice_in_dim(down_weight, core * half_down, half_down, 0),
        ],
        axis=0,
    )
    rows_half = lax.all_gather(rows_half, PLANE, axis=0, tiled=False)
    payload, columns = pin(payload, columns)
    columns = spread_columns(columns)
    w_joined = columns[:, : 4 * head_cols]
    w_up = columns[:, 4 * head_cols :]
    side = 2 * head_cols + HEAD_DIM
    table = jnp.transpose(w_joined[:, side : side + 16].astype(F32))

    payload_far = core_swap(payload)
    pos = jnp.concatenate(
        [payload[:, 2 * rows : 2 * rows + 2, :rows], payload_far[:, 2 * rows : 2 * rows + 2, :rows]]
    ).astype(F32)
    pos = (pos[:, 0] * 128.0 + pos[:, 1]).reshape(1, tokens)
    turn, spread, keep = rotary_constants()
    inv_freq = 1.0 / 10000.0 ** (jnp.arange(0, ROTARY, 2, dtype=F32) / ROTARY)
    angles = pos * inv_freq[:, None]

    def to_lanes(values):
        return lax.dot_general(values, spread, (((0,), (0,)), ((), ())), precision=HIGH)

    cosine, sine = to_lanes(jnp.cos(angles)) + keep, to_lanes(jnp.sin(angles))

    own = lax.dynamic_slice_in_dim(rows_half, core * (peers // 2), peers // 2, 0)
    far = lax.dynamic_slice_in_dim(rows_half, (1 - core) * (peers // 2), peers // 2, 0)
    halves = jnp.stack(in_order(core, own, core_swap(far)), axis=1)
    w_down = halves[:, :, half_out:].reshape(up_cols, width)
    w_out = halves[:, :, :half_out].reshape(2, HEAD_DIM, width)
    w_out = jnp.pad(w_out, ((0, 0), (HEAD_DIM, 0), (0, 0))).reshape(2 * head_cols, width)

    gain_one, gain_two = table[0], table[2]
    bias_joined = lax.dynamic_slice_in_dim(table[6:9], slice_index * head_cols, head_cols, 1)
    bias_joined = bias_joined.reshape(3, 2, HEAD_DIM)
    bias_joined = jnp.concatenate(
        [
            pair_up(bias_joined[1], bias_joined[2]),
            pair_up(bias_joined[0], jnp.zeros_like(bias_joined[0])),
        ],
        axis=0,
    ).reshape(1, -1)
    bias_up = lax.dynamic_slice_in_dim(
        jnp.transpose(table[9:13]).reshape(-1), slice_index * up_cols, up_cols, 0
    )
    which = jnp.stack([lax.axis_index("x"), core]).astype(jnp.int32)
    message, first_in, second_in, scaled, grads = front(
        which, payload, payload_far, table, bias_joined, cosine, sine, w_joined, w_out
    )

    arrived = exchange(message, PLANE)

    up_pre = jnp.dot(second_in, w_up, preferred_element_type=F32) + bias_up
    activated, gelu_pull = jax.vjp(lambda v: jax.nn.gelu(v, approximate=False), up_pre)
    activated = activated.astype(BF)
    feed = jnp.dot(activated, w_down, preferred_element_type=F32)
    grad_hidden = jnp.einsum("td,fd->tf", grads, w_down, preferred_element_type=F32)
    grad_up = gelu_pull(grad_hidden)[0].astype(BF)
    grad_second = jnp.einsum("tc,fc->tf", grad_up, w_up, preferred_element_type=F32)
    up_grad = jnp.einsum("tf,tc->fc", second_in, grad_up, preferred_element_type=F32)
    down_grad = jnp.einsum("tf,td->fd", activated, grads, preferred_element_type=F32)

    def send_columns(columns):
        return exchange(columns.reshape(planes * peers, shard_rows, -1), SHARD)

    def collect_columns(columns):
        return jnp.sum(columns.reshape(planes, peers, shard_rows, -1).astype(F32), axis=1)

    def split_rows(grad, half):
        halves = grad.astype(BF).reshape(peers // 2, 2, half, width)
        own = lax.dynamic_index_in_dim(halves, core, 1, keepdims=False)
        far = core_swap(lax.dynamic_index_in_dim(halves, 1 - core, 1, keepdims=False))
        return jnp.concatenate(in_order(core, own, far), axis=0)

    arrived, up_grad, down_rows, feed, grad_second = pin(
        arrived, up_grad.astype(BF), split_rows(down_grad, half_down), feed, grad_second
    )
    up_arrived = send_columns(up_grad)
    down_sum = lax.psum_scatter(down_rows, PLANE, scatter_dimension=0, tiled=False)
    attended, up_arrived = pin(attend(arrived, which), up_arrived)
    answered = exchange(attended, PLANE)

    block_sum, grad_scaled, joined_grad, out_grad, sums = back(
        which,
        answered,
        table,
        cosine,
        sine,
        w_joined,
        w_out,
        first_in,
        scaled,
        grads,
        feed,
        grad_second,
    )
    out_grad = out_grad.reshape(2, 2, HEAD_DIM, width)[:, 1].reshape(head_cols, width)
    out_arrived = exchange(split_rows(out_grad, half_out), PLANE)

    def other_core(total):
        total = total.reshape(2, planes, rows, width)
        own, far = total[0], core_swap(total[1])
        return (own.astype(F32) + far.astype(F32)).astype(BF)

    block_sum = other_core(block_sum)
    block_moved = [
        ring_move(
            lax.dynamic_index_in_dim(block_sum, lax.rem(plane + shift, planes), 0, keepdims=False),
            "y",
            planes,
            shift,
        )
        for shift in ring_shifts(planes)
    ]
    block_sum = lax.dynamic_index_in_dim(block_sum, plane, 0, keepdims=False).astype(F32)
    grad_scaled = other_core(grad_scaled)
    totals = jnp.concatenate([sums[:4], jnp.sum(cotangent.astype(F32), axis=0)[None]], axis=0)
    joined_sum = sums[4, : 4 * head_cols].reshape(2, 2, 2, HEAD_DIM)
    joined_sum = jnp.stack([joined_sum[1, :, 0], joined_sum[0, :, 0], joined_sum[0, :, 1]])
    bias_sums = jnp.concatenate(
        [
            jnp.transpose(joined_sum.reshape(3, head_cols)),
            jnp.sum(grad_up.astype(F32), axis=0).reshape(head_cols, -1),
        ],
        axis=1,
    )
    bias_sums = lax.dynamic_update_slice_in_dim(
        jnp.zeros((width, bias_sums.shape[1]), F32), bias_sums, slice_index * head_cols, 0
    )
    vectors = jnp.concatenate([jnp.transpose(totals), bias_sums], axis=1)
    n_vectors = vectors.shape[1]
    columns = joined_grad + jnp.pad(
        vectors, ((0, 0), (side, joined_grad.shape[1] - side - n_vectors))
    )
    columns, out_arrived = pin(columns.astype(BF), out_arrived)
    columns = send_columns(columns)
    grad_scaled, columns, down_sum, *block_moved = pin(
        grad_scaled, columns, down_sum, *block_moved
    )
    grad_scaled = exchange(grad_scaled, "y")

    def beside(part):
        part = part.reshape(2, -1, up_cols)
        return jnp.concatenate([part[0], part[1]], axis=1)

    parts = [
        beside(collect_columns(columns)),
        beside(collect_columns(up_arrived)),
        down_sum.astype(F32),
        jnp.sum(out_arrived.astype(F32), axis=0),
    ]
    part = lax.reduce_precision(jnp.concatenate(parts, axis=0), 8, 7)
    far = lax.ppermute(part.astype(BF), "zh", [(0, 1), (1, 0)])
    far, grad_scaled = pin(far, grad_scaled)
    part = part + far.astype(F32)
    joined_weight_grad, up_weight_grad, down_weight_grad, output_weight_grad, vectors = settle(
        which,
        part,
        core_swap(part),
        (
            joined_weight.shape,
            up_weight.shape,
            down_weight.shape,
            output_weight.shape,
            (shard_rows, 2 * HEAD_DIM),
        ),
    )
    grad_scaled = jnp.sum(grad_scaled.astype(F32), axis=0)

    for block in block_moved:
        block_sum = block_sum + block.astype(F32)
    inputs = hidden_in.astype(F32)
    block_out = (inputs + block_sum + (table[4] + table[5])).astype(BF)
    own_scaled, inverse = normalize(inputs)
    mean_plain = jnp.mean(grad_scaled, axis=-1, keepdims=True)
    mean_scaled = jnp.mean(grad_scaled * own_scaled, axis=-1, keepdims=True)
    input_grad = (
        cotangent.astype(F32) + inverse * (grad_scaled - mean_plain - own_scaled * mean_scaled)
    ).astype(BF)
    return (
        block_out,
        input_grad,
        vectors[:, 0],
        vectors[:, 1],
        vectors[:, 2],
        vectors[:, 3],
        joined_weight_grad,
        vectors[:, 5:8],
        output_weight_grad,
        vectors[:, 4],
        up_weight_grad,
        vectors[:, 8:12].reshape(wide_rows),
        down_weight_grad,
        vectors[:, 4],
    )


def solution(mesh):
    fine = Mesh(mesh.devices.reshape(2, 2, 4, 4, 2), AXES)
    token = P(AXES, None)
    vector = P(SHARD)
    matrix = P(SHARD, None)
    in_specs = (
        (token, P(AXES))
        + (vector,) * 4
        + (matrix, matrix, matrix, vector, matrix, vector, matrix, vector, token)
    )
    out_specs = (
        (token, token)
        + (vector,) * 4
        + (matrix, matrix, matrix, vector, matrix, vector, matrix, vector)
    )
    return jax.shard_map(
        per_device, mesh=fine, in_specs=in_specs, out_specs=out_specs, check_vma=False
    )
```

```python
import jax
import jax.numpy as jnp
import numpy as np
from jax import lax
from jax.experimental import pallas as pl
from jax.experimental.pallas import tpu as pltpu
from jax.sharding import Mesh
from jax.sharding import PartitionSpec as P

HEAD_DIM = 64
ROTARY = 16
EPS = 1e-05
NEG = -1e30
HIGH = lax.Precision.HIGHEST
MIDDLE = lax.Precision.HIGH
BF = jnp.bfloat16
F32 = jnp.float32
ROW = 128
QT = 512
KT = 512
AXES = ("zh", "c", "y", "x", "zl")
PLANE = ("x", "zl")
SHARD = ("y", "x", "zl")


def attention_kernel(which, msg, out, kv, kvt, qg, qz, gz, dkv, held, tops):
    sources, blocks = msg.shape[0], msg.shape[1]
    chunks = blocks - 2
    span = sources * ROW
    wide = 2 * HEAD_DIM
    low_rows = lax.broadcasted_iota(jnp.int32, (wide, span), 0) < HEAD_DIM
    low_lanes = lax.broadcasted_iota(jnp.int32, (ROW, wide), 1) < HEAD_DIM
    one = (
        lax.broadcasted_iota(jnp.int32, (wide, wide), 0)
        == lax.broadcasted_iota(jnp.int32, (wide, wide), 1)
    ).astype(BF)

    def turned(rows):
        return lax.dot_general(one, rows, (((1,), (1,)), ((), ())), preferred_element_type=F32)

    def key_place(place):
        chunk = lax.rem(place + which[1] * (chunks // 2), chunks)
        return pl.multiple_of(chunk * span, span)

    def load_keys(place, carry):
        at = key_place(place)
        for source in range(sources):
            kv[pl.ds(at + source * ROW, ROW), :] = msg[source, place]
        kvt[:, pl.ds(at, span)] = turned(kv[pl.ds(at, span), :]).astype(BF)
        dkv[pl.ds(at, span), :] = jnp.zeros((span, wide), F32)
        return carry

    lax.fori_loop(0, chunks, load_keys, 0)

    def load_queries(part, carry):
        at = pl.multiple_of(part * span, span)
        for source in range(sources):
            block = msg[source, chunks + part].astype(F32)
            block = jnp.where(low_lanes, block * (HEAD_DIM**-0.5), block)
            qg[pl.ds(at + source * ROW, ROW), :] = block.astype(BF)
        both = turned(qg[pl.ds(at, span), :])
        qz[:, pl.ds(at, span)] = jnp.where(low_rows, both, 0.0).astype(BF)
        gz[:, pl.ds(at, span)] = jnp.where(low_rows, 0.0, both).astype(BF)
        return carry

    lax.fori_loop(0, 2, load_queries, 0)
    lanes_tile = lax.broadcasted_iota(jnp.int32, (QT, 2 * HEAD_DIM), 1) < HEAD_DIM
    causal = lax.broadcasted_iota(jnp.int32, (KT, QT), 0) <= lax.broadcasted_iota(
        jnp.int32, (KT, QT), 1
    )
    tiles = span // QT

    def one_part(part, carry):
        chunk = jnp.where(part == which[1], which[0], chunks - 1 - which[0])
        full = chunk * tiles
        spots = [pl.multiple_of(part * span + tile * QT, QT) for tile in range(tiles)]
        query_t = [qz[:, pl.ds(at, QT)] for at in spots]
        grad_t = [gz[:, pl.ds(at, QT)] for at in spots]

        def forward(step, states, diagonal=None):
            k_at = pl.multiple_of(step * KT, KT)
            block = kv[pl.ds(k_at, KT), :]
            block_t = kvt[HEAD_DIM:, pl.ds(k_at, KT)]
            start = 0 if diagonal is None else diagonal
            scores = [
                jnp.dot(block, query_t[tile], preferred_element_type=F32)
                for tile in range(start, tiles)
            ]
            results = list(states)
            for tile in range(start, tiles):
                best, total, summed = states[tile]
                score = scores[tile - start]
                if tile == diagonal:
                    score = jnp.where(causal, score, NEG)
                new_best = jnp.maximum(best, jnp.max(score, axis=0, keepdims=True))
                probs = jnp.exp(score - new_best)
                factor = jnp.exp(best - new_best)
                total = total * factor + jnp.sum(probs, axis=0, keepdims=True)
                probs = probs.astype(BF)
                held[pl.ds(k_at, KT), tile * QT : (tile + 1) * QT] = probs
                tops[pl.ds(step, 1), tile * QT : (tile + 1) * QT] = new_best
                summed = summed * factor + jnp.dot(block_t, probs, preferred_element_type=F32)
                results[tile] = (new_best, total, summed)
            return tuple(results)

        states = tuple(
            (
                jnp.full((1, QT), NEG, F32),
                jnp.zeros((1, QT), F32),
                jnp.zeros((HEAD_DIM, QT), F32),
            )
            for _ in range(tiles)
        )
        states = lax.fori_loop(0, full, forward, states)
        for tile in range(tiles):
            states = forward(full + tile, states, tile)
        mixed, log_rows, delta, only_query, only_grad = [], [], [], [], []
        for tile, (best, total, summed) in enumerate(states):
            mixed.append((summed / total).astype(BF).astype(F32))
            log_rows.append(best + jnp.log(total))
            delta.append(
                jnp.sum(
                    mixed[tile] * grad_t[tile][HEAD_DIM:, :].astype(F32), axis=0, keepdims=True
                )
            )
            both = qg[pl.ds(spots[tile], QT), :]
            zero = jnp.zeros_like(both)
            only_query.append(jnp.where(lanes_tile, both, zero))
            only_grad.append(jnp.where(lanes_tile, zero, both))

        def backward(step, grad_query, diagonal=None):
            k_at = pl.multiple_of(step * KT, KT)
            block = kv[pl.ds(k_at, KT), :]
            block_t = kvt[:HEAD_DIM, pl.ds(k_at, KT)]
            start = 0 if diagonal is None else diagonal
            grad_probs = [
                jnp.dot(block, grad_t[tile], preferred_element_type=F32)
                for tile in range(start, tiles)
            ]
            results = list(grad_query)
            shares = []
            for tile in range(start, tiles):
                factor = jnp.exp(tops[pl.ds(step, 1), tile * QT : (tile + 1) * QT] - log_rows[tile])
                probs = held[pl.ds(k_at, KT), tile * QT : (tile + 1) * QT].astype(F32) * factor
                grad_scores = (probs * (grad_probs[tile - start] - delta[tile])).astype(BF)
                shares.append(
                    jnp.dot(grad_scores, only_query[tile], preferred_element_type=F32)
                    + jnp.dot(probs.astype(BF), only_grad[tile], preferred_element_type=F32)
                )
                results[tile] = grad_query[tile] + jnp.dot(
                    block_t, grad_scores, preferred_element_type=F32
                )
            dkv[pl.ds(k_at, KT), :] += sum(shares[1:], shares[0])
            return tuple(results)

        grad_query = tuple(jnp.zeros((HEAD_DIM, QT), F32) for _ in range(tiles))
        grad_query = lax.fori_loop(0, full, backward, grad_query)
        for tile in range(tiles):
            grad_query = backward(full + tile, grad_query, tile)
        for tile in range(tiles):
            result = jnp.concatenate([grad_query[tile] * (HEAD_DIM**-0.5), mixed[tile]], axis=0)
            result = result.T.astype(BF)
            for piece in range(QT // ROW):
                out[tile * (QT // ROW) + piece, chunks + part] = result[
                    piece * ROW : (piece + 1) * ROW
                ]
        return carry

    lax.fori_loop(0, 2, one_part, 0)

    def store_keys(place, carry):
        at = key_place(place)
        for source in range(sources):
            out[source, place] = dkv[pl.ds(at + source * ROW, ROW), :].astype(BF)
        return carry

    lax.fori_loop(0, chunks, store_keys, 0)


def attend(message, which):
    sources, blocks = message.shape[0], message.shape[1]
    keys = sources * (blocks - 2) * ROW
    queries = sources * 2 * ROW
    wide = 2 * HEAD_DIM
    pairs = keys * queries * 9 // 16
    return pl.pallas_call(
        attention_kernel,
        out_shape=jax.ShapeDtypeStruct(message.shape, BF),
        in_specs=[
            pl.BlockSpec(memory_space=pltpu.SMEM),
            pl.BlockSpec(memory_space=pltpu.VMEM),
        ],
        out_specs=pl.BlockSpec(memory_space=pltpu.VMEM),
        scratch_shapes=[
            pltpu.VMEM((keys, wide), BF),
            pltpu.VMEM((wide, keys), BF),
            pltpu.VMEM((queries, wide), BF),
            pltpu.VMEM((wide, queries), BF),
            pltpu.VMEM((wide, queries), BF),
            pltpu.VMEM((keys, wide), F32),
            pltpu.VMEM((keys, sources * ROW), BF),
            pltpu.VMEM((keys // KT, sources * ROW), F32),
        ],
        compiler_params=pltpu.CompilerParams(vmem_limit_bytes=48 * 1024 * 1024),
        cost_estimate=pl.CostEstimate(
            flops=pairs * 14 * HEAD_DIM,
            bytes_accessed=4 * sources * blocks * ROW * wide,
            transcendentals=2 * pairs,
        ),
        name="attention",
    )(which, message)


def front_kernel(
    which, own, far, table, bias, cosine, sine, w_joined, w_out, msg, first, second, scaled, grads
):
    step = pl.program_id(0)
    steps = pl.num_programs(0)
    rows = 2 * ROW
    width = own.shape[2]
    wide = 2 * HEAD_DIM
    quarters = own.shape[0] * steps // 2
    here = step < steps // 2
    values = jnp.where(here, own[:, :ROW], far[:, :ROW]).reshape(rows, width).astype(F32)
    cots = jnp.where(here, own[:, ROW : 2 * ROW], far[:, ROW : 2 * ROW]).reshape(rows, width)
    grads[...] = cots
    centered = values - jnp.mean(values, axis=-1, keepdims=True)
    variance = jnp.mean(centered * centered, axis=-1, keepdims=True)
    normal = centered * lax.rsqrt(variance + EPS)
    scaled[...] = normal
    first_in = (normal * table[0:1, :] + table[1:2, :]).astype(BF)
    first[...] = first_in
    second[...] = (normal * table[2:3, :] + table[3:4, :]).astype(BF)
    joined = jnp.dot(first_in, w_joined[...], preferred_element_type=F32) + bias[...]
    grad_mixed = lax.dot_general(
        cots, w_out[...], (((1,), (1,)), ((), ())), preferred_element_type=F32
    )
    lane = lax.broadcasted_iota(jnp.int32, (rows, wide), 1)
    half = ROTARY // 2
    for block in range(4):
        piece = joined[:, block * wide : (block + 1) * wide]
        turned = jnp.where(
            lane < half, -pltpu.roll(piece, wide - half, 1), pltpu.roll(piece, half, 1)
        )
        piece = piece * cosine[...] + turned * sine[...]
        head = block % 2
        if block >= 2:
            piece = jnp.where(lane < HEAD_DIM, piece, grad_mixed[:, head * wide : (head + 1) * wide])
        piece = piece.astype(BF)
        for i in range(2):
            place = step * 2 + i
            part = piece[i * ROW : (i + 1) * ROW]
            if block < 2:
                for quarter in range(quarters):
                    msg[quarter * 2 + head, place] = part
            else:
                later = jnp.where(here, 0, 1)
                plane = place - later * quarters
                chunk = jnp.where(later == which[1], plane, quarters - 1 - plane)
                msg[chunk * 2 + head, 2 * quarters + later] = part


def front(which, own, far, table, bias, cosine, sine, w_joined, w_out):
    planes, payload_rows, width = own.shape
    steps = planes
    rows = 2 * ROW
    tokens = 2 * planes * ROW
    wide = 2 * HEAD_DIM

    def whole(array):
        return pl.BlockSpec(array.shape, lambda s: (0,) * array.ndim)

    def rowed(columns):
        return pl.BlockSpec((rows, columns), lambda s: (s, 0))

    msg_shape = (2 * planes, 2 * planes + 2, ROW, wide)
    return pl.pallas_call(
        front_kernel,
        grid=(steps,),
        out_shape=(
            jax.ShapeDtypeStruct(msg_shape, BF),
            jax.ShapeDtypeStruct((tokens, width), BF),
            jax.ShapeDtypeStruct((tokens, width), BF),
            jax.ShapeDtypeStruct((tokens, width), F32),
            jax.ShapeDtypeStruct((tokens, width), BF),
        ),
        in_specs=[
            pl.BlockSpec(memory_space=pltpu.SMEM),
            pl.BlockSpec((2, payload_rows, width), lambda s: (jnp.minimum(s, steps // 2 - 1), 0, 0)),
            pl.BlockSpec((2, payload_rows, width), lambda s: (jnp.maximum(s - steps // 2, 0), 0, 0)),
            whole(table),
            whole(bias),
            rowed(wide),
            rowed(wide),
            whole(w_joined),
            whole(w_out),
        ],
        out_specs=(
            pl.BlockSpec(msg_shape, lambda s: (0, 0, 0, 0)),
            rowed(width),
            rowed(width),
            rowed(width),
            rowed(width),
        ),
        compiler_params=pltpu.CompilerParams(vmem_limit_bytes=48 * 1024 * 1024),
        cost_estimate=pl.CostEstimate(
            flops=2 * tokens * width * 6 * wide, bytes_accessed=24 * tokens * width, transcendentals=0
        ),
        name="front",
    )(which, own, far, table, bias, cosine, sine, w_joined, w_out)


def back_kernel(
    which,
    ans,
    table,
    cosine,
    sine,
    w_joined,
    w_out,
    first,
    scaled,
    grads,
    feed,
    second,
    block_out,
    scaled_out,
    joined_grad,
    out_grad,
    sums,
):
    step = pl.program_id(0)
    wide = 2 * HEAD_DIM
    quarters = ans.shape[0] // 2
    rows = 2 * ROW
    lane = lax.broadcasted_iota(jnp.int32, (rows, wide), 1)
    half = ROTARY // 2

    @pl.when(step == 0)
    def _():
        joined_grad[...] = jnp.zeros_like(joined_grad)
        out_grad[...] = jnp.zeros_like(out_grad)
        sums[...] = jnp.zeros_like(sums)

    def turned_back(piece):
        shifted = piece * sine[...]
        shifted = jnp.where(
            lane < half,
            pltpu.roll(shifted, wide - half, 1),
            jnp.where(lane < ROTARY, -pltpu.roll(shifted, half, 1), 0.0),
        )
        return piece * cosine[...] + shifted

    key_value, mixed, query = [], [], []
    for head in range(2):
        pair, other = [], []
        for i in range(2):
            place = step * 2 + i
            total = ans[head, place].astype(F32)
            for quarter in range(1, quarters):
                total = total + ans[quarter * 2 + head, place].astype(F32)
            pair.append(total)
            later = place // quarters
            plane = place - later * quarters
            chunk = jnp.where(later == which[1], plane, quarters - 1 - plane)
            other.append(ans[chunk * 2 + head, 2 * quarters + later])
        total = jnp.concatenate(pair, axis=0).astype(BF).astype(F32)
        key_value.append(turned_back(total).astype(BF))
        other = jnp.concatenate(other, axis=0)
        mixed.append(other)
        turned = turned_back(other.astype(F32))
        query.append(jnp.where(lane < HEAD_DIM, turned, 0.0).astype(BF))
    joined = jnp.concatenate(key_value + query, axis=1)
    mixed = jnp.concatenate(mixed, axis=1)
    cots = grads[...]
    attention = jnp.dot(mixed, w_out[...], preferred_element_type=F32)
    block_out[...] = (feed[...] + attention).astype(BF)
    grad_first = lax.dot_general(
        joined, w_joined[...], (((1,), (1,)), ((), ())), preferred_element_type=F32
    )
    grad_second = second[...]
    normal = scaled[...]
    scaled_out[...] = (grad_first * table[0:1, :] + grad_second * table[2:3, :]).astype(BF)
    over_tokens = (((0,), (0,)), ((), ()))
    joined_grad[...] += lax.dot_general(
        first[...], joined, over_tokens, preferred_element_type=F32
    )
    out_grad[...] += lax.dot_general(mixed, cots, over_tokens, preferred_element_type=F32)
    sums[0:1, :] += jnp.sum(grad_first * normal, axis=0, keepdims=True)
    sums[1:2, :] += jnp.sum(grad_first, axis=0, keepdims=True)
    sums[2:3, :] += jnp.sum(grad_second * normal, axis=0, keepdims=True)
    sums[3:4, :] += jnp.sum(grad_second, axis=0, keepdims=True)
    sums[4:5, : 4 * wide] += jnp.sum(joined.astype(F32), axis=0, keepdims=True)


def back(which, ans, table, cosine, sine, w_joined, w_out, first, scaled, grads, feed, second):
    tokens, width = scaled.shape
    rows = 2 * ROW
    wide = 2 * HEAD_DIM

    def whole(shape):
        return pl.BlockSpec(shape, lambda s: (0,) * len(shape))

    def rowed(columns):
        return pl.BlockSpec((rows, columns), lambda s: (s, 0))

    return pl.pallas_call(
        back_kernel,
        grid=(tokens // rows,),
        out_shape=(
            jax.ShapeDtypeStruct((tokens, width), BF),
            jax.ShapeDtypeStruct((tokens, width), BF),
            jax.ShapeDtypeStruct(w_joined.shape, F32),
            jax.ShapeDtypeStruct(w_out.shape, F32),
            jax.ShapeDtypeStruct((8, width), F32),
        ),
        in_specs=[pl.BlockSpec(memory_space=pltpu.SMEM), whole(ans.shape), whole(table.shape)]
        + [rowed(wide)] * 2
        + [whole(w_joined.shape), whole(w_out.shape)]
        + [rowed(width)] * 5,
        out_specs=(
            rowed(width),
            rowed(width),
            whole(w_joined.shape),
            whole(w_out.shape),
            whole((8, width)),
        ),
        compiler_params=pltpu.CompilerParams(vmem_limit_bytes=48 * 1024 * 1024),
        cost_estimate=pl.CostEstimate(
            flops=2 * tokens * width * 12 * wide, bytes_accessed=24 * tokens * width, transcendentals=0
        ),
        name="back",
    )(which, ans, table, cosine, sine, w_joined, w_out, first, scaled, grads, feed, second)


def settle_kernel(which, mine, other, joined, up, down, out, vectors, joined_bias, *norms):
    shard_rows, wide = joined.shape[0], 2 * HEAD_DIM
    planes = up.shape[1] // 1024
    up_cols = up.shape[1] // (2 * planes)
    width = joined.shape[1] // 3
    lane = lax.broadcasted_iota(jnp.int32, (shard_rows, wide), 1) < HEAD_DIM
    total = jnp.zeros((shard_rows, wide), F32)
    first = which[1] == 0
    pair = (
        jnp.where(first, mine[...], other[...]),
        jnp.where(first, other[...], mine[...]),
    )
    side = planes // 2 * shard_rows
    for core in range(2):
        source = pair[core]
        for plane in range(planes):
            top = plane % 2 * shard_rows
            left = plane // 2 * up_cols
            blocks = [
                source[top : top + shard_rows, left + i * wide : left + (i + 1) * wide]
                for i in range(4)
            ]
            at = (2 * plane + core) * wide
            swapped = [pltpu.roll(block, HEAD_DIM, 1) for block in blocks]
            joined[:, at : at + wide] = jnp.where(lane, blocks[2], swapped[3])
            joined[:, width + at : width + at + wide] = jnp.where(lane, blocks[0], swapped[1])
            joined[:, 2 * width + at : 2 * width + at + wide] = jnp.where(
                lane, swapped[0], blocks[1]
            )
            total = total + blocks[2]
            at = (2 * plane + core) * up_cols
            up[:, at : at + up_cols] = source[
                side + top : side + top + shard_rows, left : left + up_cols
            ]
        half = down.shape[0] // 2
        down[core * half : (core + 1) * half, :] = source[2 * side : 2 * side + half]
        start = 2 * side + half
        half = out.shape[0] // 2
        out[core * half : (core + 1) * half, :] = source[start : start + half]
    total = pltpu.roll(total, HEAD_DIM, 1)
    vectors[...] = total
    turned = jnp.concatenate([total] * (wide // shard_rows), axis=0).T
    joined_bias[...] = turned[5:8, :shard_rows]
    for i, norm in enumerate(norms):
        row = min(i, 4)
        norm[...] = turned[row : row + 1, :shard_rows]


def settle(which, mine, other, shapes):
    vmem = pl.BlockSpec(memory_space=pltpu.VMEM)
    return pl.pallas_call(
        settle_kernel,
        out_shape=tuple(jax.ShapeDtypeStruct(shape, F32) for shape in shapes),
        in_specs=[pl.BlockSpec(memory_space=pltpu.SMEM), vmem, vmem],
        out_specs=(vmem,) * len(shapes),
        compiler_params=pltpu.CompilerParams(vmem_limit_bytes=24 * 1024 * 1024),
        name="settle",
    )(which, mine, other)


def exchange(values, names):
    return lax.all_to_all(values, names, split_axis=0, concat_axis=0, tiled=True)


def core_swap(values):
    return lax.ppermute(values, "c", [(0, 1), (1, 0)])


def ring_shifts(size):
    return (1, size - 1, *range(2, size - 1))


def ring_move(values, names, size, shift):
    return lax.ppermute(values, names, [(i, (i + shift) % size) for i in range(size)])


def pin(*values):
    return lax.optimization_barrier(values)


def in_order(core, own, other):
    return jnp.where(core == 0, own, other), jnp.where(core == 0, other, own)


def normalize(values):
    mean = jnp.mean(values, axis=-1, keepdims=True)
    centered = values - mean
    inverse = lax.rsqrt(jnp.mean(centered * centered, axis=-1, keepdims=True) + EPS)
    return centered * inverse, inverse


def rotary_constants():
    half = ROTARY // 2
    wide = 2 * HEAD_DIM
    turn = np.zeros((wide, wide), np.float32)
    spread = np.zeros((half, wide), np.float32)
    keep = np.ones((wide,), np.float32)
    for i in range(half):
        turn[half + i, i] = -1.0
        turn[i, half + i] = 1.0
        spread[i, i] = 1.0
        spread[i, half + i] = 1.0
    keep[:ROTARY] = 0.0
    return turn, spread, keep


def per_device(
    hidden_in,
    positions,
    first_gain,
    first_shift,
    second_gain,
    second_shift,
    joined_weight,
    joined_bias,
    output_weight,
    output_bias,
    up_weight,
    up_bias,
    down_weight,
    down_bias,
    cotangent,
):
    rows, width = hidden_in.shape
    shard_rows = joined_weight.shape[0]
    hidden_width = up_weight.shape[1]
    wide_rows = down_weight.shape[0]
    planes = lax.axis_size("y")
    quarters = lax.axis_size("x")
    peers = quarters * lax.axis_size("zl")
    core = lax.axis_index("c")
    plane = lax.axis_index("y")
    tokens = 2 * planes * rows
    up_cols = hidden_width // (2 * planes)
    head_cols = width // (2 * planes)
    slice_index = 2 * plane + core

    whole = positions // 128
    pos_rows = jnp.stack([whole, positions - whole * 128]).astype(BF)
    pos_rows = jnp.pad(pos_rows, ((0, 14), (0, width - rows)))
    payload = jnp.concatenate([hidden_in, cotangent, pos_rows], axis=0)
    payload = exchange(jnp.broadcast_to(payload[None], (planes,) + payload.shape), "y")

    def pair_up(left, right):
        return jnp.concatenate([left, right], axis=-1)

    wj = lax.dynamic_index_in_dim(
        joined_weight.reshape(shard_rows, 3, planes, 2, 2, HEAD_DIM), core, 3, keepdims=False
    )
    vectors = jnp.concatenate(
        [
            jnp.stack(
                [first_gain, first_shift, second_gain, second_shift, output_bias, down_bias], axis=1
            ),
            joined_bias,
            up_bias.reshape(shard_rows, -1),
        ],
        axis=1,
    )
    vectors = jnp.pad(vectors, ((0, 0), (0, HEAD_DIM - vectors.shape[1])))
    vectors = jnp.broadcast_to(vectors[:, None, None], (shard_rows, planes, 2, HEAD_DIM))
    columns = jnp.concatenate([pair_up(wj[:, 1], wj[:, 2]), pair_up(wj[:, 0], vectors)], axis=2)
    columns = jnp.transpose(columns, (1, 0, 2, 3)).reshape(planes, shard_rows, -1)
    wu = lax.dynamic_index_in_dim(
        up_weight.reshape(shard_rows, planes, 2, up_cols), core, 2, keepdims=False
    )
    columns = jnp.concatenate([columns, jnp.transpose(wu, (1, 0, 2))], axis=2)
    half_out, half_down = shard_rows // 2, wide_rows // 2

    def spread_columns(columns):
        message = jnp.broadcast_to(columns[:, None], (planes, peers) + columns.shape[1:])
        message = exchange(message.reshape((planes * peers,) + columns.shape[1:]), SHARD)
        return message.reshape(width, -1)

    rows_half = jnp.concatenate(
        [
            lax.dynamic_slice_in_dim(output_weight, core * half_out, half_out, 0),
            lax.dynamic_slice_in_dim(down_weight, core * half_down, half_down, 0),
        ],
        axis=0,
    )
    rows_half = lax.all_gather(rows_half, PLANE, axis=0, tiled=False)
    payload, columns = pin(payload, columns)
    columns = spread_columns(columns)
    w_joined = columns[:, : 4 * head_cols]
    w_up = columns[:, 4 * head_cols :]
    side = 2 * head_cols + HEAD_DIM
    table = jnp.transpose(w_joined[:, side : side + 16].astype(F32))

    payload_far = core_swap(payload)
    pos = jnp.concatenate(
        [payload[:, 2 * rows : 2 * rows + 2, :rows], payload_far[:, 2 * rows : 2 * rows + 2, :rows]]
    ).astype(F32)
    pos = (pos[:, 0] * 128.0 + pos[:, 1]).reshape(1, tokens)
    turn, spread, keep = rotary_constants()
    inv_freq = 1.0 / 10000.0 ** (jnp.arange(0, ROTARY, 2, dtype=F32) / ROTARY)
    angles = pos * inv_freq[:, None]

    def to_lanes(values):
        return lax.dot_general(values, spread, (((0,), (0,)), ((), ())), precision=HIGH)

    cosine, sine = to_lanes(jnp.cos(angles)) + keep, to_lanes(jnp.sin(angles))

    own = lax.dynamic_slice_in_dim(rows_half, core * (peers // 2), peers // 2, 0)
    far = lax.dynamic_slice_in_dim(rows_half, (1 - core) * (peers // 2), peers // 2, 0)
    halves = jnp.stack(in_order(core, own, core_swap(far)), axis=1)
    w_down = halves[:, :, half_out:].reshape(up_cols, width)
    w_out = halves[:, :, :half_out].reshape(2, HEAD_DIM, width)
    w_out = jnp.pad(w_out, ((0, 0), (HEAD_DIM, 0), (0, 0))).reshape(2 * head_cols, width)

    gain_one, gain_two = table[0], table[2]
    bias_joined = lax.dynamic_slice_in_dim(table[6:9], slice_index * head_cols, head_cols, 1)
    bias_joined = bias_joined.reshape(3, 2, HEAD_DIM)
    bias_joined = jnp.concatenate(
        [
            pair_up(bias_joined[1], bias_joined[2]),
            pair_up(bias_joined[0], jnp.zeros_like(bias_joined[0])),
        ],
        axis=0,
    ).reshape(1, -1)
    bias_up = lax.dynamic_slice_in_dim(
        jnp.transpose(table[9:13]).reshape(-1), slice_index * up_cols, up_cols, 0
    )
    which = jnp.stack([lax.axis_index("x"), core]).astype(jnp.int32)
    message, first_in, second_in, scaled, grads = front(
        which, payload, payload_far, table, bias_joined, cosine, sine, w_joined, w_out
    )

    arrived = exchange(message, PLANE)

    up_pre = jnp.dot(second_in, w_up, preferred_element_type=F32) + bias_up
    activated, gelu_pull = jax.vjp(lambda v: jax.nn.gelu(v, approximate=False), up_pre)
    activated = activated.astype(BF)
    feed = jnp.dot(activated, w_down, preferred_element_type=F32)
    grad_hidden = jnp.einsum("td,fd->tf", grads, w_down, preferred_element_type=F32)
    grad_up = gelu_pull(grad_hidden)[0].astype(BF)
    grad_second = jnp.einsum("tc,fc->tf", grad_up, w_up, preferred_element_type=F32)
    up_grad = jnp.einsum("tf,tc->fc", second_in, grad_up, preferred_element_type=F32)
    down_grad = jnp.einsum("tf,td->fd", activated, grads, preferred_element_type=F32)

    def send_columns(columns):
        return exchange(columns.reshape(planes * peers, shard_rows, -1), SHARD)

    def collect_columns(columns):
        return jnp.sum(columns.reshape(planes, peers, shard_rows, -1).astype(F32), axis=1)

    def split_rows(grad, half):
        halves = grad.astype(BF).reshape(peers // 2, 2, half, width)
        own = lax.dynamic_index_in_dim(halves, core, 1, keepdims=False)
        far = core_swap(lax.dynamic_index_in_dim(halves, 1 - core, 1, keepdims=False))
        return jnp.concatenate(in_order(core, own, far), axis=0)

    arrived, up_grad, down_rows, feed, grad_second = pin(
        arrived, up_grad.astype(BF), split_rows(down_grad, half_down), feed, grad_second
    )
    up_arrived = send_columns(up_grad)
    attended, up_arrived, down_rows = pin(attend(arrived, which), up_arrived, down_rows)
    down_sum = lax.psum_scatter(down_rows, PLANE, scatter_dimension=0, tiled=False)
    answered = exchange(attended, PLANE)

    block_sum, grad_scaled, joined_grad, out_grad, sums = back(
        which,
        answered,
        table,
        cosine,
        sine,
        w_joined,
        w_out,
        first_in,
        scaled,
        grads,
        feed,
        grad_second,
    )
    out_grad = out_grad.reshape(2, 2, HEAD_DIM, width)[:, 1].reshape(head_cols, width)
    out_rows = split_rows(out_grad, half_out)

    def other_core(total):
        total = total.reshape(2, planes, rows, width)
        own, far = total[0], core_swap(total[1])
        return (own.astype(F32) + far.astype(F32)).astype(BF)

    block_sum = other_core(block_sum)
    block_moved = [
        ring_move(
            lax.dynamic_index_in_dim(block_sum, lax.rem(plane + shift, planes), 0, keepdims=False),
            "y",
            planes,
            shift,
        )
        for shift in ring_shifts(planes)
    ]
    block_sum = lax.dynamic_index_in_dim(block_sum, plane, 0, keepdims=False).astype(F32)
    grad_scaled = other_core(grad_scaled)
    totals = jnp.concatenate([sums[:4], jnp.sum(cotangent.astype(F32), axis=0)[None]], axis=0)
    joined_sum = sums[4, : 4 * head_cols].reshape(2, 2, 2, HEAD_DIM)
    joined_sum = jnp.stack([joined_sum[1, :, 0], joined_sum[0, :, 0], joined_sum[0, :, 1]])
    bias_sums = jnp.concatenate(
        [
            jnp.transpose(joined_sum.reshape(3, head_cols)),
            jnp.sum(grad_up.astype(F32), axis=0).reshape(head_cols, -1),
        ],
        axis=1,
    )
    bias_sums = lax.dynamic_update_slice_in_dim(
        jnp.zeros((width, bias_sums.shape[1]), F32), bias_sums, slice_index * head_cols, 0
    )
    vectors = jnp.concatenate([jnp.transpose(totals), bias_sums], axis=1)
    n_vectors = vectors.shape[1]
    columns = joined_grad + jnp.pad(
        vectors, ((0, 0), (side, joined_grad.shape[1] - side - n_vectors))
    )
    columns, out_rows = pin(send_columns(columns.astype(BF)), out_rows)
    out_arrived = exchange(out_rows, PLANE)
    grad_scaled, columns, out_arrived, down_sum, *block_moved = pin(
        grad_scaled, columns, out_arrived, down_sum, *block_moved
    )
    grad_scaled = exchange(grad_scaled, "y")

    def beside(part):
        part = part.reshape(2, -1, up_cols)
        return jnp.concatenate([part[0], part[1]], axis=1)

    parts = [
        beside(collect_columns(columns)),
        beside(collect_columns(up_arrived)),
        down_sum.astype(F32),
        jnp.sum(out_arrived.astype(F32), axis=0),
    ]
    part = lax.reduce_precision(jnp.concatenate(parts, axis=0), 8, 7)
    far = lax.ppermute(part.astype(BF), "zh", [(0, 1), (1, 0)])
    far, grad_scaled = pin(far, grad_scaled)
    part = part + far.astype(F32)
    (
        joined_weight_grad,
        up_weight_grad,
        down_weight_grad,
        output_weight_grad,
        vectors,
        joined_bias_grad,
        *norms,
    ) = settle(
        which,
        part,
        core_swap(part),
        (
            joined_weight.shape,
            up_weight.shape,
            down_weight.shape,
            output_weight.shape,
            (shard_rows, 2 * HEAD_DIM),
            joined_bias.shape[::-1],
        )
        + ((1, shard_rows),) * 6,
    )
    joined_bias_grad = jnp.transpose(joined_bias_grad)
    norms = [norm.reshape(shard_rows) for norm in norms]
    grad_scaled = jnp.sum(grad_scaled.astype(F32), axis=0)

    for block in block_moved:
        block_sum = block_sum + block.astype(F32)
    inputs = hidden_in.astype(F32)
    block_out = (inputs + block_sum + (table[4] + table[5])).astype(BF)
    own_scaled, inverse = normalize(inputs)
    mean_plain = jnp.mean(grad_scaled, axis=-1, keepdims=True)
    mean_scaled = jnp.mean(grad_scaled * own_scaled, axis=-1, keepdims=True)
    input_grad = (
        cotangent.astype(F32) + inverse * (grad_scaled - mean_plain - own_scaled * mean_scaled)
    ).astype(BF)
    return (
        block_out,
        input_grad,
        *norms[:4],
        joined_weight_grad,
        joined_bias_grad,
        output_weight_grad,
        norms[4],
        up_weight_grad,
        vectors[:, 8:12].reshape(wide_rows),
        down_weight_grad,
        norms[5],
    )


def solution(mesh):
    fine = Mesh(mesh.devices.reshape(2, 2, 4, 4, 2), AXES)
    token = P(AXES, None)
    vector = P(SHARD)
    matrix = P(SHARD, None)
    in_specs = (
        (token, P(AXES))
        + (vector,) * 4
        + (matrix, matrix, matrix, vector, matrix, vector, matrix, vector, token)
    )
    out_specs = (
        (token, token)
        + (vector,) * 4
        + (matrix, matrix, matrix, vector, matrix, vector, matrix, vector)
    )
    return jax.shard_map(
        per_device, mesh=fine, in_specs=in_specs, out_specs=out_specs, check_vma=False
    )
```

```python
import jax
import jax.numpy as jnp
import numpy as np
from jax import lax
from jax.experimental import pallas as pl
from jax.experimental.pallas import tpu as pltpu
from jax.sharding import Mesh
from jax.sharding import PartitionSpec as P

HEAD_DIM = 64
ROTARY = 16
EPS = 1e-05
NEG = -1e30
HIGH = lax.Precision.HIGHEST
MIDDLE = lax.Precision.HIGH
BF = jnp.bfloat16
F32 = jnp.float32
ROW = 128
QT = 512
KT = 512
AXES = ("zh", "c", "y", "x", "zl")
PLANE = ("x", "zl")
SHARD = ("y", "x", "zl")


def attention_kernel(which, msg, out, kv, kvt, qg, qz, gz, dkv, held, tops):
    sources, blocks = msg.shape[0], msg.shape[1]
    chunks = blocks - 2
    span = sources * ROW
    wide = 2 * HEAD_DIM
    low_rows = lax.broadcasted_iota(jnp.int32, (wide, span), 0) < HEAD_DIM
    low_lanes = lax.broadcasted_iota(jnp.int32, (ROW, wide), 1) < HEAD_DIM
    one = (
        lax.broadcasted_iota(jnp.int32, (wide, wide), 0)
        == lax.broadcasted_iota(jnp.int32, (wide, wide), 1)
    ).astype(BF)

    def turned(rows):
        return lax.dot_general(one, rows, (((1,), (1,)), ((), ())), preferred_element_type=F32)

    def key_place(place):
        chunk = lax.rem(place + which[1] * (chunks // 2), chunks)
        return pl.multiple_of(chunk * span, span)

    def load_keys(place, carry):
        at = key_place(place)
        for source in range(sources):
            kv[pl.ds(at + source * ROW, ROW), :] = msg[source, place]
        kvt[:, pl.ds(at, span)] = turned(kv[pl.ds(at, span), :]).astype(BF)
        dkv[pl.ds(at, span), :] = jnp.zeros((span, wide), F32)
        return carry

    lax.fori_loop(0, chunks, load_keys, 0)

    def load_queries(part, carry):
        at = pl.multiple_of(part * span, span)
        for source in range(sources):
            block = msg[source, chunks + part].astype(F32)
            block = jnp.where(low_lanes, block * (HEAD_DIM**-0.5), block)
            qg[pl.ds(at + source * ROW, ROW), :] = block.astype(BF)
        both = turned(qg[pl.ds(at, span), :])
        qz[:, pl.ds(at, span)] = jnp.where(low_rows, both, 0.0).astype(BF)
        gz[:, pl.ds(at, span)] = jnp.where(low_rows, 0.0, both).astype(BF)
        return carry

    lax.fori_loop(0, 2, load_queries, 0)
    lanes_tile = lax.broadcasted_iota(jnp.int32, (QT, 2 * HEAD_DIM), 1) < HEAD_DIM
    causal = lax.broadcasted_iota(jnp.int32, (KT, QT), 0) <= lax.broadcasted_iota(
        jnp.int32, (KT, QT), 1
    )
    tiles = span // QT

    def one_part(part, carry):
        chunk = jnp.where(part == which[1], which[0], chunks - 1 - which[0])
        full = chunk * tiles
        spots = [pl.multiple_of(part * span + tile * QT, QT) for tile in range(tiles)]
        query_t = [qz[:, pl.ds(at, QT)] for at in spots]
        grad_t = [gz[:, pl.ds(at, QT)] for at in spots]

        def forward(step, states, diagonal=None):
            k_at = pl.multiple_of(step * KT, KT)
            block = kv[pl.ds(k_at, KT), :]
            block_t = kvt[HEAD_DIM:, pl.ds(k_at, KT)]
            start = 0 if diagonal is None else diagonal
            scores = [
                jnp.dot(block, query_t[tile], preferred_element_type=F32)
                for tile in range(start, tiles)
            ]
            results = list(states)
            for tile in range(start, tiles):
                best, total, summed = states[tile]
                score = scores[tile - start]
                if tile == diagonal:
                    score = jnp.where(causal, score, NEG)
                new_best = jnp.maximum(best, jnp.max(score, axis=0, keepdims=True))
                probs = jnp.exp(score - new_best)
                factor = jnp.exp(best - new_best)
                total = total * factor + jnp.sum(probs, axis=0, keepdims=True)
                probs = probs.astype(BF)
                held[pl.ds(k_at, KT), tile * QT : (tile + 1) * QT] = probs
                tops[pl.ds(step, 1), tile * QT : (tile + 1) * QT] = new_best
                summed = summed * factor + jnp.dot(block_t, probs, preferred_element_type=F32)
                results[tile] = (new_best, total, summed)
            return tuple(results)

        states = tuple(
            (
                jnp.full((1, QT), NEG, F32),
                jnp.zeros((1, QT), F32),
                jnp.zeros((HEAD_DIM, QT), F32),
            )
            for _ in range(tiles)
        )
        states = lax.fori_loop(0, full, forward, states)
        for tile in range(tiles):
            states = forward(full + tile, states, tile)
        mixed, log_rows, delta, only_query, only_grad = [], [], [], [], []
        for tile, (best, total, summed) in enumerate(states):
            mixed.append((summed / total).astype(BF).astype(F32))
            log_rows.append(best + jnp.log(total))
            delta.append(
                jnp.sum(
                    mixed[tile] * grad_t[tile][HEAD_DIM:, :].astype(F32), axis=0, keepdims=True
                )
            )
            both = qg[pl.ds(spots[tile], QT), :]
            zero = jnp.zeros_like(both)
            only_query.append(jnp.where(lanes_tile, both, zero))
            only_grad.append(jnp.where(lanes_tile, zero, both))

        def backward(step, grad_query, diagonal=None):
            k_at = pl.multiple_of(step * KT, KT)
            block = kv[pl.ds(k_at, KT), :]
            block_t = kvt[:HEAD_DIM, pl.ds(k_at, KT)]
            start = 0 if diagonal is None else diagonal
            grad_probs = [
                jnp.dot(block, grad_t[tile], preferred_element_type=F32)
                for tile in range(start, tiles)
            ]
            results = list(grad_query)
            shares = []
            for tile in range(start, tiles):
                factor = jnp.exp(tops[pl.ds(step, 1), tile * QT : (tile + 1) * QT] - log_rows[tile])
                probs = held[pl.ds(k_at, KT), tile * QT : (tile + 1) * QT].astype(F32) * factor
                grad_scores = (probs * (grad_probs[tile - start] - delta[tile])).astype(BF)
                shares.append(
                    jnp.dot(grad_scores, only_query[tile], preferred_element_type=F32)
                    + jnp.dot(probs.astype(BF), only_grad[tile], preferred_element_type=F32)
                )
                results[tile] = grad_query[tile] + jnp.dot(
                    block_t, grad_scores, preferred_element_type=F32
                )
            dkv[pl.ds(k_at, KT), :] += sum(shares[1:], shares[0])
            return tuple(results)

        grad_query = tuple(jnp.zeros((HEAD_DIM, QT), F32) for _ in range(tiles))
        grad_query = lax.fori_loop(0, full, backward, grad_query)
        for tile in range(tiles):
            grad_query = backward(full + tile, grad_query, tile)
        for tile in range(tiles):
            result = jnp.concatenate([grad_query[tile] * (HEAD_DIM**-0.5), mixed[tile]], axis=0)
            result = result.T.astype(BF)
            for piece in range(QT // ROW):
                out[tile * (QT // ROW) + piece, chunks + part] = result[
                    piece * ROW : (piece + 1) * ROW
                ]
        return carry

    lax.fori_loop(0, 2, one_part, 0)

    def store_keys(place, carry):
        at = key_place(place)
        for source in range(sources):
            out[source, place] = dkv[pl.ds(at + source * ROW, ROW), :].astype(BF)
        return carry

    lax.fori_loop(0, chunks, store_keys, 0)


def attend(message, which):
    sources, blocks = message.shape[0], message.shape[1]
    keys = sources * (blocks - 2) * ROW
    queries = sources * 2 * ROW
    wide = 2 * HEAD_DIM
    pairs = keys * queries * 9 // 16
    return pl.pallas_call(
        attention_kernel,
        out_shape=jax.ShapeDtypeStruct(message.shape, BF),
        in_specs=[
            pl.BlockSpec(memory_space=pltpu.SMEM),
            pl.BlockSpec(memory_space=pltpu.VMEM),
        ],
        out_specs=pl.BlockSpec(memory_space=pltpu.VMEM),
        scratch_shapes=[
            pltpu.VMEM((keys, wide), BF),
            pltpu.VMEM((wide, keys), BF),
            pltpu.VMEM((queries, wide), BF),
            pltpu.VMEM((wide, queries), BF),
            pltpu.VMEM((wide, queries), BF),
            pltpu.VMEM((keys, wide), F32),
            pltpu.VMEM((keys, sources * ROW), BF),
            pltpu.VMEM((keys // KT, sources * ROW), F32),
        ],
        compiler_params=pltpu.CompilerParams(vmem_limit_bytes=48 * 1024 * 1024),
        cost_estimate=pl.CostEstimate(
            flops=pairs * 14 * HEAD_DIM,
            bytes_accessed=4 * sources * blocks * ROW * wide,
            transcendentals=2 * pairs,
        ),
        name="attention",
    )(which, message)


def front_kernel(
    which, own, far, table, bias, cosine, sine, w_joined, w_out, msg, first, second, scaled, grads
):
    step = pl.program_id(0)
    steps = pl.num_programs(0)
    rows = 2 * ROW
    width = own.shape[2]
    wide = 2 * HEAD_DIM
    quarters = own.shape[0] * steps // 2
    here = step < steps // 2
    values = jnp.where(here, own[:, :ROW], far[:, :ROW]).reshape(rows, width).astype(F32)
    cots = jnp.where(here, own[:, ROW : 2 * ROW], far[:, ROW : 2 * ROW]).reshape(rows, width)
    grads[...] = cots
    centered = values - jnp.mean(values, axis=-1, keepdims=True)
    variance = jnp.mean(centered * centered, axis=-1, keepdims=True)
    normal = centered * lax.rsqrt(variance + EPS)
    scaled[...] = normal
    first_in = (normal * table[0:1, :] + table[1:2, :]).astype(BF)
    first[...] = first_in
    second[...] = (normal * table[2:3, :] + table[3:4, :]).astype(BF)
    joined = jnp.dot(first_in, w_joined[...], preferred_element_type=F32) + bias[...]
    grad_mixed = lax.dot_general(
        cots, w_out[...], (((1,), (1,)), ((), ())), preferred_element_type=F32
    )
    lane = lax.broadcasted_iota(jnp.int32, (rows, wide), 1)
    half = ROTARY // 2
    for block in range(4):
        piece = joined[:, block * wide : (block + 1) * wide]
        turned = jnp.where(
            lane < half, -pltpu.roll(piece, wide - half, 1), pltpu.roll(piece, half, 1)
        )
        piece = piece * cosine[...] + turned * sine[...]
        head = block % 2
        if block >= 2:
            piece = jnp.where(lane < HEAD_DIM, piece, grad_mixed[:, head * wide : (head + 1) * wide])
        piece = piece.astype(BF)
        for i in range(2):
            place = step * 2 + i
            part = piece[i * ROW : (i + 1) * ROW]
            if block < 2:
                for quarter in range(quarters):
                    msg[quarter * 2 + head, place] = part
            else:
                later = jnp.where(here, 0, 1)
                plane = place - later * quarters
                chunk = jnp.where(later == which[1], plane, quarters - 1 - plane)
                msg[chunk * 2 + head, 2 * quarters + later] = part


def front(which, own, far, table, bias, cosine, sine, w_joined, w_out):
    planes, payload_rows, width = own.shape
    steps = planes
    rows = 2 * ROW
    tokens = 2 * planes * ROW
    wide = 2 * HEAD_DIM

    def whole(array):
        return pl.BlockSpec(array.shape, lambda s: (0,) * array.ndim)

    def rowed(columns):
        return pl.BlockSpec((rows, columns), lambda s: (s, 0))

    msg_shape = (2 * planes, 2 * planes + 2, ROW, wide)
    return pl.pallas_call(
        front_kernel,
        grid=(steps,),
        out_shape=(
            jax.ShapeDtypeStruct(msg_shape, BF),
            jax.ShapeDtypeStruct((tokens, width), BF),
            jax.ShapeDtypeStruct((tokens, width), BF),
            jax.ShapeDtypeStruct((tokens, width), F32),
            jax.ShapeDtypeStruct((tokens, width), BF),
        ),
        in_specs=[
            pl.BlockSpec(memory_space=pltpu.SMEM),
            pl.BlockSpec((2, payload_rows, width), lambda s: (jnp.minimum(s, steps // 2 - 1), 0, 0)),
            pl.BlockSpec((2, payload_rows, width), lambda s: (jnp.maximum(s - steps // 2, 0), 0, 0)),
            whole(table),
            whole(bias),
            rowed(wide),
            rowed(wide),
            whole(w_joined),
            whole(w_out),
        ],
        out_specs=(
            pl.BlockSpec(msg_shape, lambda s: (0, 0, 0, 0)),
            rowed(width),
            rowed(width),
            rowed(width),
            rowed(width),
        ),
        compiler_params=pltpu.CompilerParams(vmem_limit_bytes=48 * 1024 * 1024),
        cost_estimate=pl.CostEstimate(
            flops=2 * tokens * width * 6 * wide, bytes_accessed=24 * tokens * width, transcendentals=0
        ),
        name="front",
    )(which, own, far, table, bias, cosine, sine, w_joined, w_out)


def back_kernel(
    which,
    ans,
    table,
    cosine,
    sine,
    w_joined,
    w_out,
    first,
    scaled,
    grads,
    feed,
    second,
    block_out,
    scaled_out,
    joined_grad,
    out_grad,
    sums,
):
    step = pl.program_id(0)
    wide = 2 * HEAD_DIM
    quarters = ans.shape[0] // 2
    rows = 2 * ROW
    lane = lax.broadcasted_iota(jnp.int32, (rows, wide), 1)
    half = ROTARY // 2

    @pl.when(step == 0)
    def _():
        joined_grad[...] = jnp.zeros_like(joined_grad)
        out_grad[...] = jnp.zeros_like(out_grad)
        sums[...] = jnp.zeros_like(sums)

    def turned_back(piece):
        shifted = piece * sine[...]
        shifted = jnp.where(
            lane < half,
            pltpu.roll(shifted, wide - half, 1),
            jnp.where(lane < ROTARY, -pltpu.roll(shifted, half, 1), 0.0),
        )
        return piece * cosine[...] + shifted

    key_value, mixed, query = [], [], []
    for head in range(2):
        pair, other = [], []
        for i in range(2):
            place = step * 2 + i
            total = ans[head, place].astype(F32)
            for quarter in range(1, quarters):
                total = total + ans[quarter * 2 + head, place].astype(F32)
            pair.append(total)
            later = place // quarters
            plane = place - later * quarters
            chunk = jnp.where(later == which[1], plane, quarters - 1 - plane)
            other.append(ans[chunk * 2 + head, 2 * quarters + later])
        total = jnp.concatenate(pair, axis=0).astype(BF).astype(F32)
        key_value.append(turned_back(total).astype(BF))
        other = jnp.concatenate(other, axis=0)
        mixed.append(other)
        turned = turned_back(other.astype(F32))
        query.append(jnp.where(lane < HEAD_DIM, turned, 0.0).astype(BF))
    joined = jnp.concatenate(key_value + query, axis=1)
    mixed = jnp.concatenate(mixed, axis=1)
    cots = grads[...]
    attention = jnp.dot(mixed, w_out[...], preferred_element_type=F32)
    block_out[...] = (feed[...] + attention).astype(BF)
    grad_first = lax.dot_general(
        joined, w_joined[...], (((1,), (1,)), ((), ())), preferred_element_type=F32
    )
    grad_second = second[...]
    normal = scaled[...]
    scaled_out[...] = (grad_first * table[0:1, :] + grad_second * table[2:3, :]).astype(BF)
    over_tokens = (((0,), (0,)), ((), ()))
    joined_grad[...] += lax.dot_general(
        first[...], joined, over_tokens, preferred_element_type=F32
    )
    out_grad[...] += lax.dot_general(mixed, cots, over_tokens, preferred_element_type=F32)
    sums[0:1, :] += jnp.sum(grad_first * normal, axis=0, keepdims=True)
    sums[1:2, :] += jnp.sum(grad_first, axis=0, keepdims=True)
    sums[2:3, :] += jnp.sum(grad_second * normal, axis=0, keepdims=True)
    sums[3:4, :] += jnp.sum(grad_second, axis=0, keepdims=True)
    sums[4:5, : 4 * wide] += jnp.sum(joined.astype(F32), axis=0, keepdims=True)


def back(which, ans, table, cosine, sine, w_joined, w_out, first, scaled, grads, feed, second):
    tokens, width = scaled.shape
    rows = 2 * ROW
    wide = 2 * HEAD_DIM

    def whole(shape):
        return pl.BlockSpec(shape, lambda s: (0,) * len(shape))

    def rowed(columns):
        return pl.BlockSpec((rows, columns), lambda s: (s, 0))

    return pl.pallas_call(
        back_kernel,
        grid=(tokens // rows,),
        out_shape=(
            jax.ShapeDtypeStruct((tokens, width), BF),
            jax.ShapeDtypeStruct((tokens, width), BF),
            jax.ShapeDtypeStruct(w_joined.shape, F32),
            jax.ShapeDtypeStruct(w_out.shape, F32),
            jax.ShapeDtypeStruct((8, width), F32),
        ),
        in_specs=[pl.BlockSpec(memory_space=pltpu.SMEM), whole(ans.shape), whole(table.shape)]
        + [rowed(wide)] * 2
        + [whole(w_joined.shape), whole(w_out.shape)]
        + [rowed(width)] * 5,
        out_specs=(
            rowed(width),
            rowed(width),
            whole(w_joined.shape),
            whole(w_out.shape),
            whole((8, width)),
        ),
        compiler_params=pltpu.CompilerParams(vmem_limit_bytes=48 * 1024 * 1024),
        cost_estimate=pl.CostEstimate(
            flops=2 * tokens * width * 12 * wide, bytes_accessed=24 * tokens * width, transcendentals=0
        ),
        name="back",
    )(which, ans, table, cosine, sine, w_joined, w_out, first, scaled, grads, feed, second)


def settle_kernel(which, mine, other, joined, up, down, out, vectors, joined_bias, *norms):
    shard_rows, wide = joined.shape[0], 2 * HEAD_DIM
    planes = up.shape[1] // 1024
    up_cols = up.shape[1] // (2 * planes)
    width = joined.shape[1] // 3
    lane = lax.broadcasted_iota(jnp.int32, (shard_rows, wide), 1) < HEAD_DIM
    total = jnp.zeros((shard_rows, wide), F32)
    first = which[1] == 0
    pair = (
        jnp.where(first, mine[...], other[...]),
        jnp.where(first, other[...], mine[...]),
    )
    side = planes // 2 * shard_rows
    for core in range(2):
        source = pair[core]
        for plane in range(planes):
            top = plane % 2 * shard_rows
            left = plane // 2 * up_cols
            blocks = [
                source[top : top + shard_rows, left + i * wide : left + (i + 1) * wide]
                for i in range(4)
            ]
            at = (2 * plane + core) * wide
            swapped = [pltpu.roll(block, HEAD_DIM, 1) for block in blocks]
            joined[:, at : at + wide] = jnp.where(lane, blocks[2], swapped[3])
            joined[:, width + at : width + at + wide] = jnp.where(lane, blocks[0], swapped[1])
            joined[:, 2 * width + at : 2 * width + at + wide] = jnp.where(
                lane, swapped[0], blocks[1]
            )
            total = total + blocks[2]
            at = (2 * plane + core) * up_cols
            up[:, at : at + up_cols] = source[
                side + top : side + top + shard_rows, left : left + up_cols
            ]
        half = down.shape[0] // 2
        down[core * half : (core + 1) * half, :] = source[2 * side : 2 * side + half]
        start = 2 * side + half
        half = out.shape[0] // 2
        out[core * half : (core + 1) * half, :] = source[start : start + half]
    total = pltpu.roll(total, HEAD_DIM, 1)
    vectors[...] = total
    turned = jnp.concatenate([total] * (wide // shard_rows), axis=0).T
    joined_bias[...] = turned[5:8, :shard_rows]
    for i, norm in enumerate(norms):
        row = min(i, 4)
        norm[...] = turned[row : row + 1, :shard_rows]


def settle(which, mine, other, shapes):
    vmem = pl.BlockSpec(memory_space=pltpu.VMEM)
    return pl.pallas_call(
        settle_kernel,
        out_shape=tuple(jax.ShapeDtypeStruct(shape, F32) for shape in shapes),
        in_specs=[pl.BlockSpec(memory_space=pltpu.SMEM), vmem, vmem],
        out_specs=(vmem,) * len(shapes),
        compiler_params=pltpu.CompilerParams(vmem_limit_bytes=24 * 1024 * 1024),
        name="settle",
    )(which, mine, other)


def exchange(values, names):
    return lax.all_to_all(values, names, split_axis=0, concat_axis=0, tiled=True)


def core_swap(values):
    return lax.ppermute(values, "c", [(0, 1), (1, 0)])


def ring_shifts(size):
    return (1, size - 1, *range(2, size - 1))


def ring_move(values, names, size, shift):
    return lax.ppermute(values, names, [(i, (i + shift) % size) for i in range(size)])


def pin(*values):
    return lax.optimization_barrier(values)


def in_order(core, own, other):
    return jnp.where(core == 0, own, other), jnp.where(core == 0, other, own)


def normalize(values):
    mean = jnp.mean(values, axis=-1, keepdims=True)
    centered = values - mean
    inverse = lax.rsqrt(jnp.mean(centered * centered, axis=-1, keepdims=True) + EPS)
    return centered * inverse, inverse


def rotary_constants():
    half = ROTARY // 2
    wide = 2 * HEAD_DIM
    turn = np.zeros((wide, wide), np.float32)
    spread = np.zeros((half, wide), np.float32)
    keep = np.ones((wide,), np.float32)
    for i in range(half):
        turn[half + i, i] = -1.0
        turn[i, half + i] = 1.0
        spread[i, i] = 1.0
        spread[i, half + i] = 1.0
    keep[:ROTARY] = 0.0
    return turn, spread, keep


def per_device(
    hidden_in,
    positions,
    first_gain,
    first_shift,
    second_gain,
    second_shift,
    joined_weight,
    joined_bias,
    output_weight,
    output_bias,
    up_weight,
    up_bias,
    down_weight,
    down_bias,
    cotangent,
):
    rows, width = hidden_in.shape
    shard_rows = joined_weight.shape[0]
    hidden_width = up_weight.shape[1]
    wide_rows = down_weight.shape[0]
    planes = lax.axis_size("y")
    quarters = lax.axis_size("x")
    peers = quarters * lax.axis_size("zl")
    core = lax.axis_index("c")
    plane = lax.axis_index("y")
    tokens = 2 * planes * rows
    up_cols = hidden_width // (2 * planes)
    head_cols = width // (2 * planes)
    slice_index = 2 * plane + core

    whole = positions // 128
    pos_rows = jnp.stack([whole, positions - whole * 128]).astype(BF)
    pos_rows = jnp.pad(pos_rows, ((0, 14), (0, width - rows)))
    payload = jnp.concatenate([hidden_in, cotangent, pos_rows], axis=0)
    payload = exchange(jnp.broadcast_to(payload[None], (planes,) + payload.shape), "y")

    def pair_up(left, right):
        return jnp.concatenate([left, right], axis=-1)

    wj = lax.dynamic_index_in_dim(
        joined_weight.reshape(shard_rows, 3, planes, 2, 2, HEAD_DIM), core, 3, keepdims=False
    )
    vectors = jnp.concatenate(
        [
            jnp.stack(
                [first_gain, first_shift, second_gain, second_shift, output_bias, down_bias], axis=1
            ),
            joined_bias,
            up_bias.reshape(shard_rows, -1),
        ],
        axis=1,
    )
    vectors = jnp.pad(vectors, ((0, 0), (0, HEAD_DIM - vectors.shape[1])))
    vectors = jnp.broadcast_to(vectors[:, None, None], (shard_rows, planes, 2, HEAD_DIM))
    columns = jnp.concatenate([pair_up(wj[:, 1], wj[:, 2]), pair_up(wj[:, 0], vectors)], axis=2)
    columns = jnp.transpose(columns, (1, 0, 2, 3)).reshape(planes, shard_rows, -1)
    wu = lax.dynamic_index_in_dim(
        up_weight.reshape(shard_rows, planes, 2, up_cols), core, 2, keepdims=False
    )
    columns = jnp.concatenate([columns, jnp.transpose(wu, (1, 0, 2))], axis=2)
    half_out, half_down = shard_rows // 2, wide_rows // 2

    def spread_columns(columns):
        message = jnp.broadcast_to(columns[:, None], (planes, peers) + columns.shape[1:])
        message = exchange(message.reshape((planes * peers,) + columns.shape[1:]), SHARD)
        return message.reshape(width, -1)

    rows_half = jnp.concatenate(
        [
            lax.dynamic_slice_in_dim(output_weight, core * half_out, half_out, 0),
            lax.dynamic_slice_in_dim(down_weight, core * half_down, half_down, 0),
        ],
        axis=0,
    )
    rows_half = lax.all_gather(rows_half, PLANE, axis=0, tiled=False)
    payload, columns = pin(payload, columns)
    columns = spread_columns(columns)
    w_joined = columns[:, : 4 * head_cols]
    w_up = columns[:, 4 * head_cols :]
    side = 2 * head_cols + HEAD_DIM
    table = jnp.transpose(w_joined[:, side : side + 16].astype(F32))

    payload_far = core_swap(payload)
    pos = jnp.concatenate(
        [payload[:, 2 * rows : 2 * rows + 2, :rows], payload_far[:, 2 * rows : 2 * rows + 2, :rows]]
    ).astype(F32)
    pos = (pos[:, 0] * 128.0 + pos[:, 1]).reshape(1, tokens)
    turn, spread, keep = rotary_constants()
    inv_freq = 1.0 / 10000.0 ** (jnp.arange(0, ROTARY, 2, dtype=F32) / ROTARY)
    angles = pos * inv_freq[:, None]

    def to_lanes(values):
        return lax.dot_general(values, spread, (((0,), (0,)), ((), ())), precision=HIGH)

    cosine, sine = to_lanes(jnp.cos(angles)) + keep, to_lanes(jnp.sin(angles))

    def own_rows(gathered):
        own = lax.dynamic_slice_in_dim(gathered, core * (peers // 2), peers // 2, 0)
        far = lax.dynamic_slice_in_dim(gathered, (1 - core) * (peers // 2), peers // 2, 0)
        pair = jnp.stack(in_order(core, own, core_swap(far)), axis=1)
        return pair.reshape(peers * gathered.shape[1], width)

    w_out = own_rows(rows_half[:, :half_out]).reshape(2, HEAD_DIM, width)
    w_out = jnp.pad(w_out, ((0, 0), (HEAD_DIM, 0), (0, 0))).reshape(2 * head_cols, width)

    gain_one, gain_two = table[0], table[2]
    bias_joined = lax.dynamic_slice_in_dim(table[6:9], slice_index * head_cols, head_cols, 1)
    bias_joined = bias_joined.reshape(3, 2, HEAD_DIM)
    bias_joined = jnp.concatenate(
        [
            pair_up(bias_joined[1], bias_joined[2]),
            pair_up(bias_joined[0], jnp.zeros_like(bias_joined[0])),
        ],
        axis=0,
    ).reshape(1, -1)
    bias_up = lax.dynamic_slice_in_dim(
        jnp.transpose(table[9:13]).reshape(-1), slice_index * up_cols, up_cols, 0
    )
    which = jnp.stack([lax.axis_index("x"), core]).astype(jnp.int32)
    message, first_in, second_in, scaled, grads = front(
        which, payload, payload_far, table, bias_joined, cosine, sine, w_joined, w_out
    )
    message, rows_half = pin(message, rows_half)
    w_down = own_rows(rows_half[:, half_out:])

    arrived = exchange(message, PLANE)

    up_pre = jnp.dot(second_in, w_up, preferred_element_type=F32) + bias_up
    activated, gelu_pull = jax.vjp(lambda v: jax.nn.gelu(v, approximate=False), up_pre)
    activated = activated.astype(BF)
    feed = jnp.dot(activated, w_down, preferred_element_type=F32)
    grad_hidden = jnp.einsum("td,fd->tf", grads, w_down, preferred_element_type=F32)
    grad_up = gelu_pull(grad_hidden)[0].astype(BF)
    grad_second = jnp.einsum("tc,fc->tf", grad_up, w_up, preferred_element_type=F32)
    up_grad = jnp.einsum("tf,tc->fc", second_in, grad_up, preferred_element_type=F32)
    down_grad = jnp.einsum("tf,td->fd", activated, grads, preferred_element_type=F32)

    def send_columns(columns):
        return exchange(columns.reshape(planes * peers, shard_rows, -1), SHARD)

    def collect_columns(columns):
        return jnp.sum(columns.reshape(planes, peers, shard_rows, -1).astype(F32), axis=1)

    def split_rows(grad, half):
        halves = grad.astype(BF).reshape(peers // 2, 2, half, width)
        own = lax.dynamic_index_in_dim(halves, core, 1, keepdims=False)
        far = core_swap(lax.dynamic_index_in_dim(halves, 1 - core, 1, keepdims=False))
        return jnp.concatenate(in_order(core, own, far), axis=0)

    arrived, up_grad, down_rows, feed, grad_second = pin(
        arrived, up_grad.astype(BF), split_rows(down_grad, half_down), feed, grad_second
    )
    up_arrived = send_columns(up_grad)
    attended, up_arrived, down_rows = pin(attend(arrived, which), up_arrived, down_rows)
    down_sum = lax.psum_scatter(down_rows, PLANE, scatter_dimension=0, tiled=False)
    answered = exchange(attended, PLANE)

    block_sum, grad_scaled, joined_grad, out_grad, sums = back(
        which,
        answered,
        table,
        cosine,
        sine,
        w_joined,
        w_out,
        first_in,
        scaled,
        grads,
        feed,
        grad_second,
    )
    out_grad = out_grad.reshape(2, 2, HEAD_DIM, width)[:, 1].reshape(head_cols, width)
    out_rows = split_rows(out_grad, half_out)

    def other_core(total):
        total = total.reshape(2, planes, rows, width)
        own, far = total[0], core_swap(total[1])
        return (own.astype(F32) + far.astype(F32)).astype(BF)

    block_sum = other_core(block_sum)
    block_moved = [
        ring_move(
            lax.dynamic_index_in_dim(block_sum, lax.rem(plane + shift, planes), 0, keepdims=False),
            "y",
            planes,
            shift,
        )
        for shift in ring_shifts(planes)
    ]
    block_sum = lax.dynamic_index_in_dim(block_sum, plane, 0, keepdims=False).astype(F32)
    grad_scaled = other_core(grad_scaled)
    totals = jnp.concatenate([sums[:4], jnp.sum(cotangent.astype(F32), axis=0)[None]], axis=0)
    joined_sum = sums[4, : 4 * head_cols].reshape(2, 2, 2, HEAD_DIM)
    joined_sum = jnp.stack([joined_sum[1, :, 0], joined_sum[0, :, 0], joined_sum[0, :, 1]])
    bias_sums = jnp.concatenate(
        [
            jnp.transpose(joined_sum.reshape(3, head_cols)),
            jnp.sum(grad_up.astype(F32), axis=0).reshape(head_cols, -1),
        ],
        axis=1,
    )
    bias_sums = lax.dynamic_update_slice_in_dim(
        jnp.zeros((width, bias_sums.shape[1]), F32), bias_sums, slice_index * head_cols, 0
    )
    vectors = jnp.concatenate([jnp.transpose(totals), bias_sums], axis=1)
    n_vectors = vectors.shape[1]
    columns = joined_grad + jnp.pad(
        vectors, ((0, 0), (side, joined_grad.shape[1] - side - n_vectors))
    )
    columns, out_rows = pin(send_columns(columns.astype(BF)), out_rows)
    out_arrived = exchange(out_rows, PLANE)
    grad_scaled, columns, out_arrived, down_sum, *block_moved = pin(
        grad_scaled, columns, out_arrived, down_sum, *block_moved
    )
    grad_scaled = exchange(grad_scaled, "y")

    def beside(part):
        part = part.reshape(2, -1, up_cols)
        return jnp.concatenate([part[0], part[1]], axis=1)

    parts = [
        beside(collect_columns(columns)),
        beside(collect_columns(up_arrived)),
        down_sum.astype(F32),
        jnp.sum(out_arrived.astype(F32), axis=0),
    ]
    part = lax.reduce_precision(jnp.concatenate(parts, axis=0), 8, 7)
    far = lax.ppermute(part.astype(BF), "zh", [(0, 1), (1, 0)])
    far, grad_scaled = pin(far, grad_scaled)
    part = part + far.astype(F32)
    (
        joined_weight_grad,
        up_weight_grad,
        down_weight_grad,
        output_weight_grad,
        vectors,
        joined_bias_grad,
        *norms,
    ) = settle(
        which,
        part,
        core_swap(part),
        (
            joined_weight.shape,
            up_weight.shape,
            down_weight.shape,
            output_weight.shape,
            (shard_rows, 2 * HEAD_DIM),
            joined_bias.shape[::-1],
        )
        + ((1, shard_rows),) * 6,
    )
    joined_bias_grad = jnp.transpose(joined_bias_grad)
    norms = [norm.reshape(shard_rows) for norm in norms]
    grad_scaled = jnp.sum(grad_scaled.astype(F32), axis=0)

    for block in block_moved:
        block_sum = block_sum + block.astype(F32)
    inputs = hidden_in.astype(F32)
    block_out = (inputs + block_sum + (table[4] + table[5])).astype(BF)
    own_scaled, inverse = normalize(inputs)
    mean_plain = jnp.mean(grad_scaled, axis=-1, keepdims=True)
    mean_scaled = jnp.mean(grad_scaled * own_scaled, axis=-1, keepdims=True)
    input_grad = (
        cotangent.astype(F32) + inverse * (grad_scaled - mean_plain - own_scaled * mean_scaled)
    ).astype(BF)
    return (
        block_out,
        input_grad,
        *norms[:4],
        joined_weight_grad,
        joined_bias_grad,
        output_weight_grad,
        norms[4],
        up_weight_grad,
        vectors[:, 8:12].reshape(wide_rows),
        down_weight_grad,
        norms[5],
    )


def solution(mesh):
    fine = Mesh(mesh.devices.reshape(2, 2, 4, 4, 2), AXES)
    token = P(AXES, None)
    vector = P(SHARD)
    matrix = P(SHARD, None)
    in_specs = (
        (token, P(AXES))
        + (vector,) * 4
        + (matrix, matrix, matrix, vector, matrix, vector, matrix, vector, token)
    )
    out_specs = (
        (token, token)
        + (vector,) * 4
        + (matrix, matrix, matrix, vector, matrix, vector, matrix, vector)
    )
    return jax.shard_map(
        per_device, mesh=fine, in_specs=in_specs, out_specs=out_specs, check_vma=False
    )
```
